128 devices in a mesh: pool: 32 (over y, x, core), tensor: 4 (over z).
Axes of the slice: x: 4, y: 4, z: 4, core: 2. Of those that a mesh axis runs over, the one named last changes fastest.
Arguments:
- store: bfloat16 [384, 128, 5120], P('pool', None, 'tensor'), may hold values from -60 to 60
- new_hidden: bfloat16 [4096, 5120], P('pool', 'tensor'), may hold values from -60 to 60
- wq: bfloat16 [5120, 4096], P(None, 'tensor'), may hold values from -0.078125 to 0.078125
- wk: bfloat16 [5120, 1024], P(None, 'tensor'), may hold values from -0.078125 to 0.078125
- wv: bfloat16 [5120, 1024], P(None, 'tensor'), may hold values from -0.078125 to 0.078125
- norm_gain: float32 [5120], replicated, may hold values from 0.1 to 1.9
- q_gain: float32 [128], replicated, may hold values from 1 to 2
- k_gain: float32 [128], replicated, may hold values from 1 to 2
- page_table: int32 [32, 16], replicated, may hold values from -1 to 383, as said below
- hist_len: int32 [32], replicated, may hold values from 1 to 2048, as said below
Outputs:
- context: bfloat16 [4096, 4096], P('pool', 'tensor')
The draws below stay inside these ranges and needn't reach their ends.
Inputs may be any that keep to these rules, and one draw needn't show every extreme that they name: `page_table`: row r lists request r's history pages in order; its first ceil(hist_len[r] / 128) entries are page ids (owner id // 12, slot id % 12) and the rest are -1. Every page id appears exactly once in the table, and no request holds two pages of one owner. `hist_len`: some request has 16 full pages.
All inputs are finite; a program needn't handle non-finite values.
Results may differ from the reference program's by a relative error of at most 0.012.
Values may be sent and summed in bfloat16 or wider, within the bound.
A program may use at most 192 MiB of HBM per device.

```python
import math
import jax
import jax.numpy as jnp
from jax import lax

D = 5120
HD = 128
QH = 32
KVH = 8
PAGE = 128
NEW = 128
PG_DEV = 12
MAXPG = 16
N_POOL = 32


def feature_scales(key):
    return jnp.exp(jax.random.uniform(jax.random.fold_in(key, 5), (D,), jnp.float32, math.log(0.3), math.log(3.0)))


def page_layout(key):
    subkeys = jax.random.split(jax.random.fold_in(key, 101), 6)
    half_pool = N_POOL // 2
    first_counts = jax.random.randint(subkeys[0], (half_pool,), 2 * PG_DEV - MAXPG, MAXPG + 1)
    first_counts = first_counts.at[0].set(MAXPG)
    seq_counts = jnp.concatenate([first_counts, 2 * PG_DEV - first_counts]).astype(jnp.int32)
    seq_offsets = jnp.cumsum(seq_counts) - seq_counts
    requester_at = jax.random.permutation(subkeys[1], N_POOL).astype(jnp.int32)
    place_of = jnp.zeros((N_POOL,), jnp.int32).at[requester_at].set(jnp.arange(N_POOL, dtype=jnp.int32))
    counts = seq_counts[place_of]
    offsets = seq_offsets[place_of]
    rotation = jax.random.randint(subkeys[2], (N_POOL,), 0, MAXPG) % counts
    owner_order = jax.random.permutation(subkeys[3], N_POOL).astype(jnp.int32)
    slot_shift = jax.random.randint(subkeys[4], (N_POOL,), 0, PG_DEV)
    index = jnp.arange(MAXPG, dtype=jnp.int32)[None, :]
    sequence = offsets[:, None] + (index + rotation[:, None]) % counts[:, None]
    owner_ids = owner_order[sequence % N_POOL]
    slot_ids = (sequence // N_POOL + slot_shift[owner_ids]) % PG_DEV
    page_ids = jnp.where(index < counts[:, None], owner_ids * PG_DEV + slot_ids, -1)
    last_fill = jax.random.randint(subkeys[5], (N_POOL,), 1, PAGE + 1)
    last_fill = jnp.where(place_of == 0, PAGE, last_fill)
    lengths = (counts - 1) * PAGE + last_fill
    return (page_ids.astype(jnp.int32), lengths.astype(jnp.int32))


def draw_store(key, part):
    scales = feature_scales(key)
    key = jax.random.fold_in(key, 11)
    first_key, second_key = jax.random.split(key)
    row_count = N_POOL * PG_DEV * PAGE
    row_scale = jnp.exp(jax.random.uniform(second_key, (row_count, 1), jnp.float32, math.log(0.5), math.log(5.0)))
    base = jnp.clip(jax.random.normal(first_key, (row_count, D), jnp.float32), -4.0, 4.0)
    return (base * scales[None, :] * row_scale).reshape(N_POOL * PG_DEV, PAGE, D).astype(jnp.bfloat16)


def draw_new_hidden(key, part):
    scales = feature_scales(key)
    key = jax.random.fold_in(key, 12)
    first_key, second_key = jax.random.split(key)
    row_count = N_POOL * NEW
    row_scale = jnp.exp(jax.random.uniform(second_key, (row_count, 1), jnp.float32, math.log(0.5), math.log(5.0)))
    base = jnp.clip(jax.random.normal(first_key, (row_count, D), jnp.float32), -4.0, 4.0)
    return (base * scales[None, :] * row_scale).astype(jnp.bfloat16)


def draw_page_table(key, part):
    return page_layout(key)[0]


def draw_hist_len(key, part):
    return page_layout(key)[1]


def levels(own_key, shape, cuts, low, top_value):
    loudness, own = 1.0, jax.random.fold_in(own_key, 6)
    for axis_at, blocks in cuts:
        steps = jnp.exp(jax.random.uniform(jax.random.fold_in(own, axis_at), (blocks,), jnp.float32, low / len(cuts), top_value / len(cuts)))
        loudness = loudness * jnp.repeat(steps, shape[axis_at] // blocks).reshape([-1 if axis == axis_at else 1 for axis in range(len(shape))])
    return loudness


def scatter_about(own_key, extent, deviation, reach, cuts=(), kind=jnp.bfloat16):
    values = jax.random.normal(own_key, extent, jnp.float32) * deviation
    if len(cuts) > 0:
        values = levels(own_key, extent, cuts, -0.22, 0.18) * values
    return jnp.clip(values, min=-reach, max=reach).astype(kind)


def setup_inputs(seed: int = 0) -> dict:
    streams_of = jax.random.split(jax.random.key(seed), 11)
    store = draw_store(jax.random.fold_in(streams_of[10], 71), 0)
    new_hidden = draw_new_hidden(jax.random.fold_in(streams_of[10], 71), 0)
    wq = scatter_about(streams_of[2], (D, QH * HD), D ** -0.5, 0.078125, ((1, 4),))
    wk = scatter_about(streams_of[3], (D, KVH * HD), D ** -0.5, 0.078125, ((1, 4),))
    wv = scatter_about(streams_of[4], (D, KVH * HD), D ** -0.5, 0.078125, ((1, 4),))
    norm_gain = jnp.clip(1.0 + 0.18 * jax.random.normal(streams_of[5], (D,), jnp.float32), 0.1, 1.9)
    q_gain = jnp.clip(jnp.exp(jax.random.uniform(streams_of[6], (HD,), jnp.float32, math.log(1.0), math.log(2.0))), 1.0, 2.0)
    k_gain = jnp.clip(jnp.exp(jax.random.uniform(streams_of[7], (HD,), jnp.float32, math.log(1.0), math.log(2.0))), 1.0, 2.0)
    page_table = draw_page_table(jax.random.fold_in(streams_of[10], 71), 0)
    hist_len = draw_hist_len(jax.random.fold_in(streams_of[10], 71), 0)
    return dict(store=store, new_hidden=new_hidden, wq=wq, wk=wk, wv=wv, norm_gain=norm_gain, q_gain=q_gain, k_gain=k_gain, page_table=page_table, hist_len=hist_len)


epsilon = 1e-06
rope_base = 1000000.0

def rms_rows(row_block, gain_vec):
    values = row_block.astype(jnp.float32)
    inv_rms = lax.rsqrt(lax.optimization_barrier(jnp.mean(values * values, axis=-1, keepdims=True)) + epsilon)
    return (values * inv_rms * gain_vec).astype(jnp.bfloat16)

def head_norm(values, gain_vec):
    inv_rms = lax.rsqrt(lax.optimization_barrier(jnp.mean(values * values, axis=-1, keepdims=True)) + epsilon)
    return values * inv_rms * gain_vec

def rotate(values, positions):
    half_width = values.shape[-1] // 2
    exponent = jnp.arange(half_width, dtype=jnp.float32) * (2.0 / values.shape[-1])
    frequency = jnp.power(jnp.float32(rope_base), -exponent)
    angles = positions.astype(jnp.float32)[:, None] * frequency[None, :]
    cosine = jnp.cos(angles)[:, None, :]
    sine_part = jnp.sin(angles)[:, None, :]
    first = values[..., :half_width]
    second = values[..., half_width:]
    return jnp.concatenate([first * cosine - second * sine_part, second * cosine + first * sine_part], axis=-1)

def reference(store, new_hidden, wq, wk, wv, norm_gain, q_gain, k_gain, page_table, hist_len):
    stored_normed = rms_rows(store.reshape(-1, D), norm_gain)
    store_keys = head_norm(jnp.dot(stored_normed, wk, preferred_element_type=jnp.float32).reshape(-1, PAGE, KVH, HD), k_gain)
    store_values = jnp.dot(stored_normed, wv, preferred_element_type=jnp.float32).astype(jnp.bfloat16).reshape(-1, PAGE, KVH, HD)
    new_normed = rms_rows(new_hidden, norm_gain)
    queries_all = head_norm(jnp.dot(new_normed, wq, preferred_element_type=jnp.float32).reshape(N_POOL, NEW, QH, HD), q_gain)
    new_keys_all = head_norm(jnp.dot(new_normed, wk, preferred_element_type=jnp.float32).reshape(N_POOL, NEW, KVH, HD), k_gain)
    new_values_all = jnp.dot(new_normed, wv, preferred_element_type=jnp.float32).astype(jnp.bfloat16).reshape(N_POOL, NEW, KVH, HD)
    history = MAXPG * PAGE

    def one_request(request):
        page_ids = jnp.maximum(page_table[request], 0)
        length = hist_len[request]
        hist_pos = jnp.arange(history, dtype=jnp.int32)
        keys_hist = rotate(store_keys[page_ids].reshape(history, KVH, HD), hist_pos).astype(jnp.bfloat16)
        values_hist = store_values[page_ids].reshape(history, KVH, HD)
        new_pos = length + jnp.arange(NEW, dtype=jnp.int32)
        keys_new = rotate(new_keys_all[request], new_pos).astype(jnp.bfloat16)
        queries = rotate(queries_all[request], new_pos).astype(jnp.bfloat16)
        key_rows = jnp.concatenate([keys_hist, keys_new], axis=0)
        value_rows = jnp.concatenate([values_hist, new_values_all[request]], axis=0)
        grouped = queries.reshape(NEW, KVH, QH // KVH, HD).astype(jnp.float32)
        scores = jnp.einsum('qkgd,skd->kgqs', grouped, key_rows.astype(jnp.float32)) * HD ** (-0.5)
        key_index = jnp.arange(history + NEW, dtype=jnp.int32)[None, :]
        query_index = jnp.arange(NEW, dtype=jnp.int32)[:, None]
        allowed = jnp.where(key_index < history, key_index < length, key_index - history <= query_index)
        raw = jnp.where(allowed, jnp.exp(scores), jnp.float32(0.0))
        denominator = lax.optimization_barrier(jnp.sum(raw, axis=-1, keepdims=True))
        weights = (raw / denominator).astype(jnp.bfloat16)
        mixed = jnp.einsum('kgqs,skd->qkgd', weights.astype(jnp.float32), value_rows.astype(jnp.float32))
        return mixed.reshape(NEW, QH * HD).astype(jnp.bfloat16)
    outputs = lax.map(one_request, jnp.arange(N_POOL, dtype=jnp.int32))
    return outputs.reshape(N_POOL * NEW, QH * HD)
```

```python
import jax
import jax.numpy as jnp
import numpy as np
from jax import lax
from jax.experimental import pallas as pl
from jax.experimental.pallas import tpu as pltpu
from jax.sharding import PartitionSpec as P

EPS = 1e-06
ROPE_BASE = 1000000.0
MESH = pl.DeviceIdType.MESH
F32 = jnp.float32
BF16 = jnp.bfloat16

PAGES = 12
ROWS = 128
FEAT = 1280
NZ = 4
WIDE = FEAT * NZ
HD = 128
GROUP = 4
QROWS = GROUP * ROWS
REQS = 32
ITEMS = 12
HALF = 272
SEG = 160
SCALE = HD ** -0.5


def rope_tables():
    freq = ROPE_BASE ** (-np.arange(64, dtype=np.float64) * 2.0 / HD)
    freq = np.concatenate([freq, freq])[None, :]
    rows = np.arange(ROWS, dtype=np.float64)[:, None] * freq
    pages = np.arange(24, dtype=np.float64)[:, None] * ROWS * freq
    return [np.asarray(t, np.float32) for t in (np.cos(rows), np.sin(rows), np.cos(pages), np.sin(pages))]


class Ring:
    def __init__(self, piece, half, at, dev_up, dev_down, send, recv):
        self.piece, self.half, self.at = piece, half, at
        self.up, self.down, self.send, self.recv = dev_up, dev_down, send, recv
        self.left = lax.rem(at + 3, 4)
        self.right = lax.rem(at + 1, 4)
        self.opp = lax.rem(at + 2, 4)

    def copy(self, ref, k, dev):
        return pltpu.make_async_remote_copy(
            src_ref=ref, dst_ref=ref, send_sem=self.send(k), recv_sem=self.recv(k), device_id=dev, device_id_type=MESH
        )

    def start(self):
        self.copy(self.piece(self.at), 0, self.up).start()
        self.copy(self.piece(self.at), 1, self.down).start()

    def forward_left(self):
        self.copy(self.piece(self.left), 0, self.up).wait_recv()
        self.copy(self.half(self.left, 0), 2, self.up).start()

    def forward_right(self):
        self.copy(self.piece(self.right), 1, self.down).wait_recv()
        self.copy(self.half(self.right, 1), 3, self.down).start()

    def finish(self):
        self.copy(self.half(self.opp, 0), 2, self.up).wait_recv()
        self.copy(self.half(self.opp, 1), 3, self.down).wait_recv()

    def drain(self):
        self.copy(self.piece(self.at), 0, self.up).wait_send()
        self.copy(self.piece(self.at), 1, self.down).wait_send()
        self.copy(self.half(self.left, 0), 2, self.up).wait_send()
        self.copy(self.half(self.right, 1), 3, self.down).wait_send()


def nt(a, b):
    return lax.dot_general(a, b, (((1,), (1,)), ((), ())), preferred_element_type=F32)


def nn(a, b):
    return jnp.dot(a, b, preferred_element_type=F32)


def kernel(
    tab, store, new_hidden, wq, wk, wv, gain, q_gain, k_gain, cosr, sinr, cosp, sinp,
    out,
    X, W, WQB, WKB, WVB, ACC, NH, SSQ, INV, OPPS, OPPR, MIDS, MIDR, KB, VB, NEWCTX, QALL, CTX,
    S0, R0, S1O, R1O, S1M, R1M, A1, S2O, R2O, S2M, R2M, FIN,
    lsem, wbsem, w1s, w1r, w2s, w2r, w3s, w3r, nhs, nhr, sqs, sqr, os_, or_, ms, mr,
    q1s, q1r, q2s, q2r, q3s, q3r, c0s, c0r, c1os, c1or, c1ms, c1mr, c2os, c2or, c2ms, c2mr,
):
    p = lax.axis_index("pool")
    z = lax.axis_index("tensor")
    c = lax.rem(p, 2)
    x = lax.rem(p // 2, 4)
    y = p // 8
    oc = 1 - c

    def at(yy, xx, cc):
        return yy * 8 + xx * 2 + cc

    def rot(v, d):
        return lax.rem(v + d, 4)

    zdev = [(p, rot(z, d)) for d in range(4)]
    xup, xdn = (at(y, rot(x, 1), c), z), (at(y, rot(x, 3), c), z)
    yup, ydn = (at(rot(y, 1), x, c), z), (at(rot(y, 3), x, c), z)
    sib = (at(y, x, oc), z)

    def rcopy(src, dst, ss, rs, dev):
        return pltpu.make_async_remote_copy(
            src_ref=src, dst_ref=dst, send_sem=ss, recv_sem=rs, device_id=dev, device_id_type=MESH
        )

    ld_new = pltpu.make_async_copy(new_hidden, NH.at[z], lsem.at[0])
    ld_new.start()
    ld_x = pltpu.make_async_copy(store, X, lsem.at[1])
    ld_x.start()

    def block_loads(d):
        rows = pl.ds(pl.multiple_of(rot(z, d) * FEAT, FEAT), FEAT)
        b = d % 2
        return [
            pltpu.make_async_copy(wq.at[rows, :], WQB.at[b], wbsem.at[b, 0]),
            pltpu.make_async_copy(wk.at[rows, :], WKB.at[b], wbsem.at[b, 1]),
            pltpu.make_async_copy(wv.at[rows, :], WVB.at[b], wbsem.at[b, 2]),
        ]

    for d in (0, 1):
        for cp in block_loads(d):
            cp.start()
    own_rows = pl.ds(pl.multiple_of(z * FEAT, FEAT), FEAT)
    ld_w = []
    for h in range(2):
        for kv, ref in enumerate((wk, wv)):
            ld_w.append(
                pltpu.make_async_copy(
                    ref.at[own_rows, h * HD : (h + 1) * HD], W.at[0, h, kv], lsem.at[2 + 2 * h + kv]
                )
            )
    for cp in ld_w:
        cp.start()

    barrier = pltpu.get_barrier_semaphore()
    peers = [zdev[1], zdev[2], zdev[3], xup, xdn, yup, ydn, sib]
    for dev in peers:
        pl.semaphore_signal(barrier, inc=1, device_id=dev, device_id_type=MESH)
    pl.semaphore_wait(barrier, len(peers))

    ring_at = (x, y)

    def seg_rows(cc, k):
        return pl.ds(pl.multiple_of(cc * (4 * SEG) + k * SEG, SEG), SEG)

    def w1_copy(e, h, kv):
        ref = (wk, wv)[kv]
        seg = pl.multiple_of(c * (4 * SEG) + ring_at[kv] * SEG, SEG)
        src = ref.at[pl.ds(pl.multiple_of(rot(z, e) * FEAT + seg, SEG), SEG), h * HD : (h + 1) * HD]
        return rcopy(src, W.at[4 - e, h, kv, pl.ds(seg, SEG), :], w1s.at[kv, h, e], w1r.at[kv, h, 4 - e], zdev[e])

    for kv in range(2):
        for h in range(2):
            for e in (2, 1, 3):
                w1_copy(e, h, kv).start()

    def w1_wait(slot, h, kv):
        seg = pl.multiple_of(c * (4 * SEG) + ring_at[kv] * SEG, SEG)
        dst = W.at[slot, h, kv, pl.ds(seg, SEG), :]
        rcopy(dst, dst, w1s.at[kv, h, slot], w1r.at[kv, h, slot], zdev[slot]).wait_recv()

    lane = lax.broadcasted_iota(jnp.int32, (ROWS, ROWS), 1)
    row = lax.broadcasted_iota(jnp.int32, (ROWS, ROWS), 0)
    eye = lane == row

    def squares_of(v):
        v = v.astype(F32)
        return jnp.sum(v * v, axis=1, keepdims=True)

    ld_new.wait()
    squares = jnp.where(lane == PAGES, squares_of(NH[z]), 0.0)
    ld_x.wait()
    squares = lax.fori_loop(0, PAGES, lambda j, acc: jnp.where(lane == j, squares_of(X[j]), acc), squares)
    SSQ[z] = jnp.transpose(squares)[:16, :]
    for e in (1, 2, 3):
        rcopy(SSQ.at[z], SSQ.at[z], sqs.at[e], sqr.at[e], zdev[e]).start()
    for e in (1, 2, 3):
        far = SSQ.at[rot(z, 4 - e)]
        rcopy(far, far, sqs.at[e], sqr.at[e], zdev[e]).wait_recv()
    total = SSQ[0] + SSQ[1] + SSQ[2] + SSQ[3]
    inverse = lax.rsqrt(total * (1.0 / WIDE) + EPS)
    INV[...] = jnp.transpose(jnp.concatenate([inverse, jnp.zeros((ROWS - 16, ROWS), F32)], axis=0))

    def normed(v, j):
        inv = jnp.sum(jnp.where(lane == j, INV[...], 0.0), axis=1, keepdims=True)
        return (v.astype(F32) * inv * gain[...]).astype(BF16)

    NH[z] = normed(NH[z], PAGES)
    nh_ring = Ring(
        lambda k: NH.at[k], lambda k, s: NH.at[k, pl.ds(64 * s, 64), :], z, zdev[1], zdev[3],
        lambda k: nhs.at[k], lambda k: nhr.at[k],
    )
    nh_ring.start()

    def prepare(j, carry):
        X[j] = normed(X[j], j)
        return carry

    lax.fori_loop(0, PAGES, prepare, 0)

    def w_piece(kv, cc):
        return lambda k: W.at[pl.ds(1, 3), :, kv, seg_rows(cc, k), :]

    def w_half(kv):
        def half(k, s):
            first = pl.multiple_of(c * (4 * SEG) + k * SEG + s * (SEG // 2), SEG // 2)
            return W.at[pl.ds(1, 3), :, kv, pl.ds(first, SEG // 2), :]

        return half

    def w_ring_of(kv, up, down):
        return Ring(
            w_piece(kv, c), w_half(kv), ring_at[kv], up, down, lambda k: w2s.at[kv, k], lambda k: w2r.at[kv, k]
        )

    w_rings = [w_ring_of(0, xup, xdn), w_ring_of(1, yup, ydn)]

    def w3_copy(kv, cc, k, n):
        ref = w_piece(kv, cc)(k)
        return rcopy(ref, ref, w3s.at[kv, n], w3r.at[kv, n], sib)

    for kv in range(2):
        for h in range(2):
            for slot in (1, 2, 3):
                w1_wait(slot, h, kv)
        w_rings[kv].start()
        w3_copy(kv, c, ring_at[kv], 0).start()
    nh_ring.forward_left()
    nh_ring.forward_right()
    for kv in range(2):
        w_rings[kv].forward_left()
        w3_copy(kv, c, w_rings[kv].left, 1).start()
        w_rings[kv].forward_right()
        w3_copy(kv, c, w_rings[kv].right, 2).start()

    sign = jnp.where(lax.broadcasted_iota(jnp.int32, (1, HD), 1) < HD // 2, -1.0, 1.0).astype(F32)
    cos_r, sin_r = cosr[...], sinr[...]

    def angle_at(first_cos, first_sin):
        return first_cos * cos_r - first_sin * sin_r, (first_sin * cos_r + first_cos * sin_r) * sign

    def normed_rope(v, g, cos, sin):
        v = v * lax.rsqrt(jnp.mean(v * v, axis=1, keepdims=True) + EPS) * g
        return (v * cos + pltpu.roll(v, HD // 2, 1) * sin).astype(BF16)

    def project_new(d):
        for cp in block_loads(d):
            cp.wait()
        b = d % 2
        a = NH[rot(z, d)]
        parts = ((0, WQB), (1024, WKB), (1280, WVB))
        for first, ref in parts:
            width = ref.shape[2]
            prod = nn(a, ref[b])
            if d == 0:
                ACC[:, first : first + width] = prod
            else:
                ACC[:, first : first + width] += prod
        if d < 2:
            for cp in block_loads(d + 2):
                cp.start()

    project_new(0)
    project_new(1)
    nh_ring.finish()
    project_new(2)
    project_new(3)
    page_cos, page_sin = cosp[pl.ds(tab[5, 0], 1), :], sinp[pl.ds(tab[5, 0], 1), :]
    rest_cos, rest_sin = cosr[pl.ds(tab[5, 1], 1), :], sinr[pl.ds(tab[5, 1], 1), :]
    cos_new, sin_new = angle_at(
        page_cos * rest_cos - page_sin * rest_sin, page_sin * rest_cos + page_cos * rest_sin
    )
    q_at = (c * 16 + y * 4 + x, c * 16 + x * 4 + y)
    for h in range(2):
        for g in range(GROUP):
            n = h * GROUP + g
            raw = ACC[:, n * HD : (n + 1) * HD]
            QALL[h, q_at[h], g * ROWS : (g + 1) * ROWS, :] = normed_rope(raw, q_gain[...], cos_new, sin_new)

    def q1_ring_of(h):
        base = c * 16 + (y * 4, x * 4)[h]
        up, down = ((xup, xdn), (yup, ydn))[h]
        return Ring(
            lambda k: QALL.at[h, base + k],
            lambda k, s: QALL.at[h, base + k, pl.ds(s * 256, 256), :],
            (x, y)[h], up, down, lambda k: q1s.at[h, k], lambda k: q1r.at[h, k],
        )

    def q2_ring_of(h):
        up, down = ((yup, ydn), (xup, xdn))[h]
        return Ring(
            lambda k: QALL.at[h, pl.ds(c * 16 + k * 4, 4)],
            lambda k, s: QALL.at[h, pl.ds(c * 16 + k * 4 + s * 2, 2)],
            (y, x)[h], up, down, lambda k: q2s.at[h, k], lambda k: q2r.at[h, k],
        )

    q1 = [q1_ring_of(h) for h in range(2)]
    q2 = [q2_ring_of(h) for h in range(2)]

    def q3_copy(h, cc, k, n):
        ref = QALL.at[h, pl.ds(cc * 16 + k * 4, 4)]
        return rcopy(ref, ref, q3s.at[h, n], q3r.at[h, n], sib)

    for h in range(2):
        q1[h].start()

    causal = lax.broadcasted_iota(jnp.int32, (QROWS, ROWS), 1) <= (
        lax.broadcasted_iota(jnp.int32, (QROWS, ROWS), 0) & (ROWS - 1)
    )
    ones = jnp.ones((ROWS, HD), BF16)
    for h in range(2):
        raw = ACC[:, 1024 + h * HD : 1024 + (h + 1) * HD]
        key = normed_rope(raw, k_gain[...], cos_new, sin_new)
        val = (ACC[:, 1280 + h * HD : 1280 + (h + 1) * HD]).astype(BF16)
        scores = nt(QALL[h, q_at[h]], key) * SCALE
        weights = jnp.where(causal, jnp.exp(scores), 0.0).astype(BF16)
        NEWCTX[h] = nn(weights, jnp.concatenate([val, ones], axis=1))

    for kv in range(2):
        w_rings[kv].finish()
        w3_copy(kv, c, w_rings[kv].opp, 3).start()
    for kv in range(2):
        for n, k in enumerate((ring_at[kv], w_rings[kv].left, w_rings[kv].right, w_rings[kv].opp)):
            w3_copy(kv, oc, k, n).wait_recv()
    for cp in ld_w:
        cp.wait()

    def product(i, slot):
        h, pair = i // 6, lax.rem(i, 6)
        a = X[pl.ds(pair * 2, 2)].reshape(2 * ROWS, FEAT)
        return nn(a, jnp.concatenate([W[slot, h, 0], W[slot, h, 1]], axis=1))

    def opp_copy(i, s):
        return rcopy(OPPS.at[i, s], OPPR.at[i, s], os_.at[i, s], or_.at[i, s], (zdev[1], zdev[3])[s])

    def mid_copy(i, s):
        return rcopy(MIDS.at[i, s], MIDR.at[i, s], ms.at[i, s], mr.at[i, s], (zdev[1], zdev[3])[s])

    def opposite(i):
        part = product(i, 2).astype(BF16)
        for s in range(2):
            OPPS[i, s] = part[s * ROWS : (s + 1) * ROWS]
            opp_copy(i, s).start()

    def neighbours(i):
        for s in range(2):
            part = product(i, (1, 3)[s])
            opp_copy(i, s).wait_recv()
            for t in range(2):
                page = part[t * ROWS : (t + 1) * ROWS]
                if t == s:
                    page = page + OPPR[i, s].astype(F32)
                MIDS[i, s, t] = page.astype(BF16)
            mid_copy(i, s).start()

    def own(i):
        h, pair = i // 6, lax.rem(i, 6)
        part = product(i, 0)
        for s in range(2):
            mid_copy(i, s).wait_recv()
        for t in range(2):
            j = pair * 2 + t
            page = part[t * ROWS : (t + 1) * ROWS] + MIDR[i, 0, t].astype(F32) + MIDR[i, 1, t].astype(F32)
            n = h * PAGES + j
            i_page = tab[2, j]
            cos, sin = angle_at(cosp[pl.ds(i_page, 1), :], sinp[pl.ds(i_page, 1), :])
            KB[n] = normed_rope(page[:, :HD], k_gain[...], cos, sin)
            live = row < tab[3, j]
            VB[n, :, :HD] = jnp.where(live, page[:, HD:], 0.0).astype(BF16)
            VB[n, :, HD:] = jnp.where(live, 1.0, 0.0).astype(BF16)

    def attend(n, carry):
        h, j = n // PAGES, lax.rem(n, PAGES)
        scores = nt(QALL[h, tab[h, j]], KB[n]) * SCALE
        mixed = nn(jnp.exp(scores).astype(BF16), VB[n])
        line = lax.broadcasted_iota(jnp.int32, (16, HD), 0)
        for s in range(2):
            CTX[h, j, s, :256, :] = mixed[s * 256 : (s + 1) * 256, :HD].astype(BF16)
            sums = []
            for g in range(2):
                block = mixed[s * 256 + g * ROWS : s * 256 + (g + 1) * ROWS, HD:]
                sums.append(jnp.sum(jnp.where(eye, block, 0.0), axis=0, keepdims=True))
            CTX[h, j, s, 256:, :] = jnp.where(line == 0, sums[0], jnp.where(line == 1, sums[1], 0.0)).astype(BF16)
        return carry

    first_dev = ((xup, xdn), (yup, ydn))
    last_dev = ((yup, ydn), (xup, xdn))
    first_at, last_at = (x, y), (y, x)

    def piece_at(s, a, b):
        return b * 4 + a if s == 0 else a * 4 + b

    def value(h, s, a, b):
        q = piece_at(s, a, b)
        return CTX[h, tab[4, q * 2 + c], s].astype(F32) + R0[h, q, s].astype(F32)

    def c0_copy(h):
        return rcopy(S0, R0.at[h], c0s.at[h], c0r.at[h], sib)

    def c0(h):
        def fill(q, carry):
            S0[q] = CTX[h, tab[4, q * 2 + oc]]
            return carry

        lax.fori_loop(0, 16, fill, 0)
        c0_copy(h).start()

    def c1o_copy(h, s, d):
        part = pl.ds(d * 2, 2)
        return rcopy(S1O.at[h, s, part], R1O.at[h, s, part], c1os.at[h, s, d], c1or.at[h, s, d], first_dev[s][d])

    def c1m_copy(h, s, d):
        return rcopy(S1M.at[h, s, d], R1M.at[h, s, d], c1ms.at[h, s, d], c1mr.at[h, s, d], first_dev[s][d])

    cuts = (pl.ds(0, 128), pl.ds(128, HALF - 128))

    def c2o_copy(h, s, d):
        return rcopy(
            S2O.at[h, s, cuts[d]], R2O.at[h, s, cuts[d]], c2os.at[h, s, d], c2or.at[h, s, d], last_dev[s][d]
        )

    def c2m_copy(h, s, d):
        return rcopy(S2M.at[h, s, d], R2M.at[h, s, d], c2ms.at[h, s, d], c2mr.at[h, s, d], last_dev[s][d])

    def c1(h):
        c0_copy(h).wait_recv()
        for s in range(2):
            a = rot(first_at[s], 2)

            def fill(b, carry):
                S1O[h, s, b] = value(h, s, a, b).astype(BF16)
                return carry

            lax.fori_loop(0, 4, fill, 0)
            for d in range(2):
                c1o_copy(h, s, d).start()

    def c2(h):
        for d in range(2):
            for s in range(2):
                a = rot(first_at[s], (1, 3)[d])
                c1o_copy(h, s, d).wait_recv()

                def with_far(b, carry):
                    S1M[h, s, d, b] = (value(h, s, a, b) + R1O[h, s, b].astype(F32)).astype(BF16)
                    return carry

                def without(b, carry):
                    S1M[h, s, d, b] = value(h, s, a, b).astype(BF16)
                    return carry

                lax.fori_loop(d * 2, d * 2 + 2, with_far, 0)
                lax.fori_loop(2 - d * 2, 4 - d * 2, without, 0)
                c1m_copy(h, s, d).start()

    def c3(h):
        for s in range(2):
            for d in range(2):
                c1m_copy(h, s, d).wait_recv()

            def fill(b, carry):
                A1[s, b] = value(h, s, first_at[s], b) + R1M[h, s, 0, b].astype(F32) + R1M[h, s, 1, b].astype(F32)
                return carry

            lax.fori_loop(0, 4, fill, 0)
            S2O[h, s] = A1[s, rot(last_at[s], 2)].astype(BF16)
            for d in range(2):
                c2o_copy(h, s, d).start()

    def c4(h):
        for s in range(2):
            for d in range(2):
                c2o_copy(h, s, d).wait_recv()
                mine = A1[s, rot(last_at[s], (1, 3)[d])]
                far = R2O[h, s, cuts[d], :].astype(F32)
                if d == 0:
                    total = jnp.concatenate([mine[:128] + far, mine[128:]], axis=0)
                else:
                    total = jnp.concatenate([mine[:128], mine[128:] + far], axis=0)
                S2M[h, s, d] = total.astype(BF16)
                c2m_copy(h, s, d).start()

    def c5(h):
        for s in range(2):
            for d in range(2):
                c2m_copy(h, s, d).wait_recv()
            FIN[...] = A1[s, last_at[s]] + R2M[h, s, 0].astype(F32) + R2M[h, s, 1].astype(F32)
            for g in range(2):
                n = s * 2 + g
                mixed = FIN[g * ROWS : (g + 1) * ROWS, :] + NEWCTX[h, n * ROWS : (n + 1) * ROWS, :HD]
                sums = jnp.sum(jnp.where(eye, FIN[256 + g : 257 + g, :], 0.0), axis=1, keepdims=True)
                sums = sums + NEWCTX[h, n * ROWS : (n + 1) * ROWS, HD:]
                m = h * GROUP + n
                out[:, m * HD : (m + 1) * HD] = (mixed / sums).astype(BF16)

    CTX[0, PAGES] = jnp.zeros((2, HALF, HD), BF16)
    CTX[1, PAGES] = jnp.zeros((2, HALF, HD), BF16)

    def step(i, carry):
        @pl.when(i < ITEMS)
        def _():
            opposite(i)

        @pl.when(jnp.logical_and(i >= 1, i <= ITEMS))
        def _():
            neighbours(i - 1)

        @pl.when(i >= 2)
        def _():
            own(i - 2)

        @pl.when(i == 1)
        def _():
            for h in range(2):
                q1[h].forward_left()
                q1[h].forward_right()

        @pl.when(i == 2)
        def _():
            for h in range(2):
                q1[h].finish()
                q2[h].start()
                q3_copy(h, c, (y, x)[h], 0).start()

        @pl.when(i == 5)
        def _():
            for h in range(2):
                q2[h].forward_left()
                q3_copy(h, c, q2[h].left, 1).start()
                q2[h].forward_right()
                q3_copy(h, c, q2[h].right, 2).start()

        @pl.when(i == 6)
        def _():
            for h in range(2):
                q2[h].finish()
                q3_copy(h, c, q2[h].opp, 3).start()

        @pl.when(i == 7)
        def _():
            for h in range(2):
                for n, k in enumerate((q2[h].at, q2[h].left, q2[h].right, q2[h].opp)):
                    q3_copy(h, oc, k, n).wait_recv()
            lax.fori_loop(0, PAGES, attend, 0)
            c0(0)

        @pl.when(i >= 8)
        def _():
            lax.fori_loop(2 * (i - 2), 2 * (i - 1), attend, 0)

        for k, stage in ((8, c1), (9, c2), (10, c3), (11, c4), (12, c5)):

            @pl.when(i == k)
            def _(stage=stage):
                stage(0)

        return carry

    lax.fori_loop(0, ITEMS + 2, step, 0)
    c0_copy(0).wait_send()
    for stage in (c0, c1, c2, c3, c4, c5):
        stage(1)

    c0_copy(1).wait_send()
    for kv in range(2):
        for h in range(2):
            for e in (1, 2, 3):
                w1_copy(e, h, kv).wait_send()
        w_rings[kv].drain()
        for n, k in enumerate((ring_at[kv], w_rings[kv].left, w_rings[kv].right, w_rings[kv].opp)):
            w3_copy(kv, c, k, n).wait_send()
    nh_ring.drain()
    for e in (1, 2, 3):
        rcopy(SSQ.at[z], SSQ.at[z], sqs.at[e], sqr.at[e], zdev[e]).wait_send()

    def drain(i, carry):
        for s in range(2):
            opp_copy(i, s).wait_send()
            mid_copy(i, s).wait_send()
        return carry

    lax.fori_loop(0, ITEMS, drain, 0)
    for h in range(2):
        q1[h].drain()
        q2[h].drain()
        for n, k in enumerate((q2[h].at, q2[h].left, q2[h].right, q2[h].opp)):
            q3_copy(h, c, k, n).wait_send()
        for s in range(2):
            for d in range(2):
                c1o_copy(h, s, d).wait_send()
                c1m_copy(h, s, d).wait_send()
                c2o_copy(h, s, d).wait_send()
                c2m_copy(h, s, d).wait_send()


def local(store, new_hidden, wq, wk, wv, norm_gain, q_gain, k_gain, page_table, hist_len):
    p = lax.axis_index("pool")
    z = lax.axis_index("tensor")
    flat = page_table.reshape(1, -1)
    entry = jnp.arange(flat.shape[1], dtype=jnp.int32)[None, :]
    request, place = entry // 16, entry % 16
    room = jnp.clip(jnp.repeat(hist_len, 16)[None, :] - place * ROWS, 0, ROWS)
    listed = flat == p * PAGES + jnp.arange(32, dtype=jnp.int32)[:, None]
    listed = jnp.logical_and(listed, jnp.arange(32, dtype=jnp.int32)[:, None] < PAGES)

    def pick(v):
        return jnp.sum(jnp.where(listed, v, 0), axis=1)

    page_request = pick(request)
    core, xx, yy = page_request % 2, (page_request // 2) % 4, page_request // 8
    mine = jnp.logical_and(page_table >= 0, page_table // PAGES == p)
    slot = PAGES + jnp.sum(jnp.where(mine, page_table % PAGES - PAGES, 0), axis=1)
    length = jnp.broadcast_to(lax.dynamic_index_in_dim(hist_len, p, 0, keepdims=False), (32,))
    first = jnp.arange(32) == 0
    tab = jnp.stack(
        [
            core * 16 + yy * 4 + xx,
            core * 16 + xx * 4 + yy,
            pick(place),
            pick(room),
            slot,
            jnp.where(first, length // ROWS, length % ROWS),
        ]
    ).astype(jnp.int32)
    gain = lax.dynamic_slice_in_dim(norm_gain, z * FEAT, FEAT, 0).reshape(1, FEAT)
    tables = [jnp.asarray(t) for t in rope_tables()]
    vm = pl.BlockSpec(memory_space=pltpu.VMEM)
    hbm = pl.BlockSpec(memory_space=pl.ANY)
    dma = pltpu.SemaphoreType.DMA
    scratch = [
        pltpu.VMEM((PAGES, ROWS, FEAT), BF16),
        pltpu.VMEM((4, 2, 2, FEAT, HD), BF16),
        pltpu.VMEM((2, FEAT, 1024), BF16),
        pltpu.VMEM((2, FEAT, 256), BF16),
        pltpu.VMEM((2, FEAT, 256), BF16),
        pltpu.VMEM((ROWS, 1536), F32),
        pltpu.VMEM((4, ROWS, FEAT), BF16),
        pltpu.VMEM((4, 16, ROWS), F32),
        pltpu.VMEM((ROWS, ROWS), F32),
        pltpu.VMEM((ITEMS, 2, ROWS, 256), BF16),
        pltpu.VMEM((ITEMS, 2, ROWS, 256), BF16),
        pltpu.VMEM((ITEMS, 2, 2, ROWS, 256), BF16),
        pltpu.VMEM((ITEMS, 2, 2, ROWS, 256), BF16),
        pltpu.VMEM((2 * PAGES, ROWS, HD), BF16),
        pltpu.VMEM((2 * PAGES, ROWS, 2 * HD), BF16),
        pltpu.VMEM((2, QROWS, 2 * HD), F32),
        pltpu.VMEM((2, REQS, QROWS, HD), BF16),
        pltpu.VMEM((2, PAGES + 1, 2, HALF, HD), BF16),
        pltpu.VMEM((16, 2, HALF, HD), BF16),
        pltpu.VMEM((2, 16, 2, HALF, HD), BF16),
        pltpu.VMEM((2, 2, 4, HALF, HD), BF16),
        pltpu.VMEM((2, 2, 4, HALF, HD), BF16),
        pltpu.VMEM((2, 2, 2, 4, HALF, HD), BF16),
        pltpu.VMEM((2, 2, 2, 4, HALF, HD), BF16),
        pltpu.VMEM((2, 4, HALF, HD), F32),
        pltpu.VMEM((2, 2, HALF, HD), BF16),
        pltpu.VMEM((2, 2, HALF, HD), BF16),
        pltpu.VMEM((2, 2, 2, HALF, HD), BF16),
        pltpu.VMEM((2, 2, 2, HALF, HD), BF16),
        pltpu.VMEM((HALF, HD), F32),
        dma((6,)), dma((2, 3)),
        dma((2, 2, 4)), dma((2, 2, 4)), dma((2, 4)), dma((2, 4)), dma((2, 4)), dma((2, 4)),
        dma((4,)), dma((4,)), dma((4,)), dma((4,)),
        dma((ITEMS, 2)), dma((ITEMS, 2)), dma((ITEMS, 2)), dma((ITEMS, 2)),
        dma((2, 4)), dma((2, 4)), dma((2, 4)), dma((2, 4)), dma((2, 4)), dma((2, 4)),
        dma((2,)), dma((2,)),
        dma((2, 2, 2)), dma((2, 2, 2)), dma((2, 2, 2)), dma((2, 2, 2)),
        dma((2, 2, 2)), dma((2, 2, 2)), dma((2, 2, 2)), dma((2, 2, 2)),
    ]
    return pl.pallas_call(
        kernel,
        out_shape=jax.ShapeDtypeStruct((ROWS, 2 * GROUP * HD), BF16),
        in_specs=[pl.BlockSpec(memory_space=pltpu.SMEM)] + [hbm] * 5 + [vm] * 7,
        out_specs=vm,
        scratch_shapes=scratch,
        compiler_params=pltpu.CompilerParams(
            collective_id=0, has_side_effects=True, vmem_limit_bytes=63 * 1024 * 1024
        ),
        cost_estimate=pl.CostEstimate(flops=12_000_000_000, bytes_accessed=25_000_000, transcendentals=2_000_000),
    )(tab, store, new_hidden, wq, wk, wv, gain, q_gain.reshape(1, HD), k_gain.reshape(1, HD), *tables)


def solution(mesh):
    return jax.shard_map(
        local,
        mesh=mesh,
        in_specs=(
            P("pool", None, "tensor"),
            P("pool", "tensor"),
            P(None, "tensor"),
            P(None, "tensor"),
            P(None, "tensor"),
            P(),
            P(),
            P(),
            P(),
            P(),
        ),
        out_specs=P("pool", "tensor"),
        check_vma=False,
    )
```

```python
import jax
import jax.numpy as jnp
import numpy as np
from jax import lax
from jax.experimental import pallas as pl
from jax.experimental.pallas import tpu as pltpu
from jax.sharding import PartitionSpec as P

EPS = 1e-06
ROPE_BASE = 1000000.0
MESH = pl.DeviceIdType.MESH
F32 = jnp.float32
BF16 = jnp.bfloat16

PAGES = 12
ROWS = 128
FEAT = 1280
NZ = 4
WIDE = FEAT * NZ
HD = 128
GROUP = 4
QROWS = GROUP * ROWS
REQS = 32
ITEMS = 12
HALF = 272
SEG = 160
SCALE = HD ** -0.5


def rope_tables():
    freq = ROPE_BASE ** (-np.arange(64, dtype=np.float64) * 2.0 / HD)
    freq = np.concatenate([freq, freq])[None, :]
    rows = np.arange(ROWS, dtype=np.float64)[:, None] * freq
    pages = np.arange(24, dtype=np.float64)[:, None] * ROWS * freq
    return [np.asarray(t, np.float32) for t in (np.cos(rows), np.sin(rows), np.cos(pages), np.sin(pages))]


class Ring:
    def __init__(self, piece, half, at, dev_up, dev_down, send, recv):
        self.piece, self.half, self.at = piece, half, at
        self.up, self.down, self.send, self.recv = dev_up, dev_down, send, recv
        self.left = lax.rem(at + 3, 4)
        self.right = lax.rem(at + 1, 4)
        self.opp = lax.rem(at + 2, 4)

    def copy(self, ref, k, dev):
        return pltpu.make_async_remote_copy(
            src_ref=ref, dst_ref=ref, send_sem=self.send(k), recv_sem=self.recv(k), device_id=dev, device_id_type=MESH
        )

    def start(self):
        self.copy(self.piece(self.at), 0, self.up).start()
        self.copy(self.piece(self.at), 1, self.down).start()

    def forward_left(self):
        self.copy(self.piece(self.left), 0, self.up).wait_recv()
        self.copy(self.half(self.left, 0), 2, self.up).start()

    def forward_right(self):
        self.copy(self.piece(self.right), 1, self.down).wait_recv()
        self.copy(self.half(self.right, 1), 3, self.down).start()

    def finish(self):
        self.copy(self.half(self.opp, 0), 2, self.up).wait_recv()
        self.copy(self.half(self.opp, 1), 3, self.down).wait_recv()

    def drain(self):
        self.copy(self.piece(self.at), 0, self.up).wait_send()
        self.copy(self.piece(self.at), 1, self.down).wait_send()
        self.copy(self.half(self.left, 0), 2, self.up).wait_send()
        self.copy(self.half(self.right, 1), 3, self.down).wait_send()


def nt(a, b):
    return lax.dot_general(a, b, (((1,), (1,)), ((), ())), preferred_element_type=F32)


def nn(a, b):
    return jnp.dot(a, b, preferred_element_type=F32)


def kernel(
    table, lengths, store, new_hidden, wq, wk, wv, norm_gain, q_gain, k_gain, cosr, sinr, cosp, sinp,
    out,
    X, W, WQB, WKB, WVB, ACC, NH, SSQ, INV, OPPS, OPPR, MIDS, MIDR, KB, VB, NEWCTX, QA, QB, CTX,
    S0, R0, S1O, R1O, S1M, R1M, A1, S2O, R2O, S2M, R2M, FIN, TV, TS,
    lsem, wbsem, w1s, w1r, w2s, w2r, w3s, w3r, nhs, nhr, sqs, sqr, os_, or_, ms, mr,
    q1s, q1r, q2s, q2r, q3s, q3r, c0s, c0r, c1os, c1or, c1ms, c1mr, c2os, c2or, c2ms, c2mr,
):
    QS = (QA, QB)
    p = lax.axis_index("pool")
    z = lax.axis_index("tensor")
    c = lax.rem(p, 2)
    x = lax.rem(p // 2, 4)
    y = p // 8
    oc = 1 - c

    def at(yy, xx, cc):
        return yy * 8 + xx * 2 + cc

    def rot(v, d):
        return lax.rem(v + d, 4)

    zdev = [(p, rot(z, d)) for d in range(4)]
    xup, xdn = (at(y, rot(x, 1), c), z), (at(y, rot(x, 3), c), z)
    yup, ydn = (at(rot(y, 1), x, c), z), (at(rot(y, 3), x, c), z)
    sib = (at(y, x, oc), z)

    def rcopy(src, dst, ss, rs, dev):
        return pltpu.make_async_remote_copy(
            src_ref=src, dst_ref=dst, send_sem=ss, recv_sem=rs, device_id=dev, device_id_type=MESH
        )

    ld_new = pltpu.make_async_copy(new_hidden, NH.at[z], lsem.at[0])
    ld_new.start()
    ld_x = [pltpu.make_async_copy(store.at[pl.ds(6 * n, 6)], X.at[pl.ds(6 * n, 6)], lsem.at[1 + n]) for n in range(2)]
    for cp in ld_x:
        cp.start()

    barrier = pltpu.get_barrier_semaphore()
    peers = [zdev[1], zdev[2], zdev[3], xup, xdn, yup, ydn, sib]
    for dev in peers:
        pl.semaphore_signal(barrier, inc=1, device_id=dev, device_id_type=MESH)

    page = table[...] - p * PAGES
    hit = jnp.logical_and(page >= 0, page < PAGES)
    rank = lax.broadcasted_iota(jnp.int32, (16, REQS), 0)
    slots = PAGES + jnp.sum(jnp.where(hit, page - PAGES, 0), axis=0, keepdims=True)
    askers = jnp.where(slots == rank, lax.broadcasted_iota(jnp.int32, (16, REQS), 1), 0)
    TV[...] = jnp.zeros_like(TV)
    TV[0:1, :REQS] = jnp.clip(slots, 0, PAGES)
    TV[1:2, :REQS] = jnp.clip(jnp.sum(jnp.where(hit, rank, 0), axis=0, keepdims=True), 0, 15)
    TV[8:24, :] = jnp.broadcast_to(jnp.clip(jnp.sum(askers, axis=1, keepdims=True), 0, REQS - 1), (16, HD))
    to_scalar = pltpu.make_async_copy(TV, TS, lsem.at[3])
    to_scalar.start()

    CTX[0, PAGES] = jnp.zeros((2, HALF, HD), BF16)
    CTX[1, PAGES] = jnp.zeros((2, HALF, HD), BF16)

    lane = lax.broadcasted_iota(jnp.int32, (ROWS, ROWS), 1)
    row = lax.broadcasted_iota(jnp.int32, (ROWS, ROWS), 0)
    eye = lane == row
    gain = jnp.concatenate([norm_gain[pl.ds(z * (FEAT // HD) + k, 1), :] for k in range(FEAT // HD)], axis=1)

    def squares_of(v):
        v = v.astype(F32)
        return jnp.sum(v * v, axis=1, keepdims=True)

    ld_new.wait()
    squares = jnp.where(lane == PAGES, squares_of(NH[z]), 0.0)
    for n in range(2):
        ld_x[n].wait()
        squares = lax.fori_loop(
            6 * n, 6 * n + 6, lambda j, acc: jnp.where(lane == j, squares_of(X[j]), acc), squares
        )
    SSQ[z] = jnp.transpose(squares)[:16, :]
    to_scalar.wait()

    def block_loads(d):
        rows = pl.ds(pl.multiple_of(rot(z, d) * FEAT, FEAT), FEAT)
        b = (0, 1, 1, 0)[d]
        return [
            pltpu.make_async_copy(wq.at[rows, :], WQB.at[b], wbsem.at[b, 0]),
            pltpu.make_async_copy(wk.at[rows, :], WKB.at[b], wbsem.at[b, 1]),
            pltpu.make_async_copy(wv.at[rows, :], WVB.at[b], wbsem.at[b, 2]),
        ]

    own_rows = pl.ds(pl.multiple_of(z * FEAT, FEAT), FEAT)
    ld_w = []
    for h in range(2):
        for kv, ref in enumerate((wk, wv)):
            ld_w.append(
                pltpu.make_async_copy(
                    ref.at[own_rows, h * HD : (h + 1) * HD], W.at[0, h, kv], lsem.at[4 + 2 * h + kv]
                )
            )

    pl.semaphore_wait(barrier, len(peers))
    for e in (1, 2, 3):
        rcopy(SSQ.at[z], SSQ.at[z], sqs.at[e], sqr.at[e], zdev[e]).start()

    ring_at = (x, y)

    def seg_rows(cc, k):
        return pl.ds(pl.multiple_of(cc * (4 * SEG) + k * SEG, SEG), SEG)

    def w1_copy(e, h, kv):
        ref = (wk, wv)[kv]
        seg = pl.multiple_of(c * (4 * SEG) + ring_at[kv] * SEG, SEG)
        src = ref.at[pl.ds(pl.multiple_of(rot(z, e) * FEAT + seg, SEG), SEG), h * HD : (h + 1) * HD]
        return rcopy(src, W.at[4 - e, h, kv, pl.ds(seg, SEG), :], w1s.at[kv, h, e], w1r.at[kv, h, 4 - e], zdev[e])

    for h in range(2):
        for kv in range(2):
            for e in (2, 1, 3):
                w1_copy(e, h, kv).start()

    def w1_wait(slot, h, kv):
        seg = pl.multiple_of(c * (4 * SEG) + ring_at[kv] * SEG, SEG)
        dst = W.at[slot, h, kv, pl.ds(seg, SEG), :]
        rcopy(dst, dst, w1s.at[kv, h, slot], w1r.at[kv, h, slot], zdev[slot]).wait_recv()

    for d in (0, 1):
        for cp in block_loads(d):
            cp.start()
    for cp in ld_w:
        cp.start()

    for e in (1, 2, 3):
        far = SSQ.at[rot(z, 4 - e)]
        rcopy(far, far, sqs.at[e], sqr.at[e], zdev[e]).wait_recv()
    total = SSQ[0] + SSQ[1] + SSQ[2] + SSQ[3]
    inverse = lax.rsqrt(total * (1.0 / WIDE) + EPS)
    INV[...] = jnp.transpose(jnp.concatenate([inverse, jnp.zeros((ROWS - 16, ROWS), F32)], axis=0))

    def normed(v, j):
        inv = jnp.sum(jnp.where(lane == j, INV[...], 0.0), axis=1, keepdims=True)
        return (v.astype(F32) * inv * gain).astype(BF16)

    NH[z] = normed(NH[z], PAGES)
    nh_ring = Ring(
        lambda k: NH.at[k], lambda k, s: NH.at[k, pl.ds(64 * s, 64), :], z, zdev[1], zdev[3],
        lambda k: nhs.at[k], lambda k: nhr.at[k],
    )
    nh_ring.start()

    def prepare(j, carry):
        X[j] = normed(X[j], j)
        return carry

    lax.fori_loop(0, PAGES, prepare, 0)

    def w_piece(h, kv, cc):
        return lambda k: W.at[pl.ds(1, 3), h, kv, seg_rows(cc, k), :]

    def w_half(h, kv):
        def half(k, s):
            first = pl.multiple_of(c * (4 * SEG) + k * SEG + s * (SEG // 2), SEG // 2)
            return W.at[pl.ds(1, 3), h, kv, pl.ds(first, SEG // 2), :]

        return half

    def w_ring_of(h, kv):
        up, down = ((xup, xdn), (yup, ydn))[kv]
        return Ring(
            w_piece(h, kv, c), w_half(h, kv), ring_at[kv], up, down,
            lambda k: w2s.at[h, kv, k], lambda k: w2r.at[h, kv, k],
        )

    w_rings = [[w_ring_of(h, kv) for kv in range(2)] for h in range(2)]

    def w3_copy(h, kv, cc, n):
        ring = w_rings[h][kv]
        ref = w_piece(h, kv, cc)((ring.at, ring.left, ring.right, ring.opp)[n])
        return rcopy(ref, ref, w3s.at[h, kv, n], w3r.at[h, kv, n], sib)

    def w_start(h):
        for kv in range(2):
            for slot in (1, 2, 3):
                w1_wait(slot, h, kv)
            w_rings[h][kv].start()
            w3_copy(h, kv, c, 0).start()

    def w_forward(h):
        for kv in range(2):
            w_rings[h][kv].forward_left()
            w3_copy(h, kv, c, 1).start()
            w_rings[h][kv].forward_right()
            w3_copy(h, kv, c, 2).start()

    def w_finish(h):
        for kv in range(2):
            w_rings[h][kv].finish()
            w3_copy(h, kv, c, 3).start()

    def w_wait(h):
        for kv in range(2):
            for n in range(4):
                w3_copy(h, kv, oc, n).wait_recv()
            ld_w[2 * h + kv].wait()

    sign = jnp.where(lax.broadcasted_iota(jnp.int32, (1, HD), 1) < HD // 2, -1.0, 1.0).astype(F32)
    cos_r, sin_r = cosr[...], sinr[...]

    def angle_at(first_cos, first_sin):
        return first_cos * cos_r - first_sin * sin_r, (first_sin * cos_r + first_cos * sin_r) * sign

    def normed_rope(v, g, cos, sin):
        v = v * lax.rsqrt(jnp.mean(v * v, axis=1, keepdims=True) + EPS) * g
        return (v * cos + pltpu.roll(v, HD // 2, 1) * sin).astype(BF16)

    def project_new(d):
        for cp in block_loads(d):
            cp.wait()
        b = (0, 1, 1, 0)[d]
        a = NH[rot(z, d)]
        parts = ((0, WQB), (1024, WKB), (1280, WVB))
        for first, ref in parts:
            width = ref.shape[2]
            prod = nn(a, ref[b])
            if d == 0:
                ACC[:, first : first + width] = prod
            else:
                ACC[:, first : first + width] += prod
        if d < 2:
            for cp in block_loads(3 - d):
                cp.start()

    w_start(0)
    project_new(0)
    w_start(1)
    w_forward(0)
    nh_ring.forward_left()
    nh_ring.forward_right()
    project_new(1)
    project_new(3)
    w_finish(0)
    w_forward(1)
    w_wait(0)

    def product(i, slot):
        h, pair = i // 6, lax.rem(i, 6)
        a = X[pl.ds(pair * 2, 2)].reshape(2 * ROWS, FEAT)
        return nn(a, jnp.concatenate([W[slot, h, 0], W[slot, h, 1]], axis=1))

    def opp_copy(i, s):
        return rcopy(OPPS.at[i, s], OPPR.at[i, s], os_.at[i, s], or_.at[i, s], (zdev[1], zdev[3])[s])

    def mid_copy(i, s):
        return rcopy(MIDS.at[i, s], MIDR.at[i, s], ms.at[i, s], mr.at[i, s], (zdev[1], zdev[3])[s])

    def opposite(i):
        part = product(i, 2).astype(BF16)
        for s in range(2):
            OPPS[i, s] = part[s * ROWS : (s + 1) * ROWS]
            opp_copy(i, s).start()

    def neighbours(i):
        for s in range(2):
            part = product(i, (1, 3)[s])
            opp_copy(i, s).wait_recv()
            for t in range(2):
                page = part[t * ROWS : (t + 1) * ROWS]
                if t == s:
                    page = page + OPPR[i, s].astype(F32)
                MIDS[i, s, t] = page.astype(BF16)
            mid_copy(i, s).start()

    def own(i):
        h, pair = i // 6, lax.rem(i, 6)
        part = product(i, 0)
        for s in range(2):
            mid_copy(i, s).wait_recv()
        for t in range(2):
            j = pair * 2 + t
            page = part[t * ROWS : (t + 1) * ROWS] + MIDR[i, 0, t].astype(F32) + MIDR[i, 1, t].astype(F32)
            n = h * PAGES + j
            request = TS[8 + j, 0]
            i_page = TS[1, request]
            cos, sin = angle_at(cosp[pl.ds(i_page, 1), :], sinp[pl.ds(i_page, 1), :])
            KB[n] = normed_rope(page[:, :HD], k_gain[...], cos, sin)
            live = row < lengths[request] - i_page * ROWS
            VB[n, :, :HD] = jnp.where(live, page[:, HD:], 0.0).astype(BF16)
            VB[n, :, HD:] = jnp.where(live, 1.0, 0.0).astype(BF16)

    def attend(h, j):
        n = h * PAGES + j
        request = TS[8 + j, 0]
        core, xx, yy = lax.rem(request, 2), lax.rem(request // 2, 4), request // 8
        query = jnp.concatenate(
            [QS[h][0, core * 16 + yy * 4 + xx], QS[h][1, core * 16 + xx * 4 + yy]], axis=0
        )
        scores = nt(query, KB[n]) * SCALE
        mixed = nn(jnp.exp(scores).astype(BF16), VB[n])
        line = lax.broadcasted_iota(jnp.int32, (16, HD), 0)
        for s in range(2):
            CTX[h, j, s, :256, :] = mixed[s * 256 : (s + 1) * 256, :HD].astype(BF16)
            sums = []
            for g in range(2):
                block = mixed[s * 256 + g * ROWS : s * 256 + (g + 1) * ROWS, HD:]
                sums.append(jnp.sum(jnp.where(eye, block, 0.0), axis=0, keepdims=True))
            CTX[h, j, s, 256:, :] = jnp.where(line == 0, sums[0], jnp.where(line == 1, sums[1], 0.0)).astype(BF16)

    def attend_pages(h, first, last):
        def one(j, carry):
            attend(h, j)
            return carry

        lax.fori_loop(first, last, one, 0)

    opposite(0)
    opposite(1)
    w_finish(1)
    nh_ring.finish()
    project_new(2)
    length = lengths[p]
    page_cos, page_sin = cosp[pl.ds(length // ROWS, 1), :], sinp[pl.ds(length // ROWS, 1), :]
    rest_cos, rest_sin = cosr[pl.ds(lax.rem(length, ROWS), 1), :], sinr[pl.ds(lax.rem(length, ROWS), 1), :]
    cos_new, sin_new = angle_at(
        page_cos * rest_cos - page_sin * rest_sin, page_sin * rest_cos + page_cos * rest_sin
    )

    q_at = (c * 16 + y * 4 + x, c * 16 + x * 4 + y)

    def q1_ring_of(h, s):
        base = c * 16 + (y * 4, x * 4)[s]
        up, down = ((xup, xdn), (yup, ydn))[s]
        return Ring(
            lambda k: QS[h].at[s, base + k],
            lambda k, t: QS[h].at[s, base + k, pl.ds(t * 128, 128), :],
            (x, y)[s], up, down, lambda k: q1s.at[h, s, k], lambda k: q1r.at[h, s, k],
        )

    def q2_ring_of(h, s):
        up, down = ((yup, ydn), (xup, xdn))[s]
        return Ring(
            lambda k: QS[h].at[s, pl.ds(c * 16 + k * 4, 4)],
            lambda k, t: QS[h].at[s, pl.ds(c * 16 + k * 4 + t * 2, 2)],
            (y, x)[s], up, down, lambda k: q2s.at[h, s, k], lambda k: q2r.at[h, s, k],
        )

    q1 = [[q1_ring_of(h, s) for s in range(2)] for h in range(2)]
    q2 = [[q2_ring_of(h, s) for s in range(2)] for h in range(2)]

    def q3_copy(h, s, cc, n):
        k = (q2[h][s].at, q2[h][s].left, q2[h][s].right, q2[h][s].opp)[n]
        ref = QS[h].at[s, pl.ds(cc * 16 + k * 4, 4)]
        return rcopy(ref, ref, q3s.at[h, s, n], q3r.at[h, s, n], sib)

    for h in range(2):
        for s in range(2):
            for g in range(2):
                n = h * GROUP + s * 2 + g
                raw = ACC[:, n * HD : (n + 1) * HD]
                QS[h][s, q_at[s], g * ROWS : (g + 1) * ROWS, :] = normed_rope(raw, q_gain[...], cos_new, sin_new)
            q1[h][s].start()

    def q1_forward(h):
        for s in range(2):
            q1[h][s].forward_left()
            q1[h][s].forward_right()

    def q2_start(h):
        for s in range(2):
            q1[h][s].finish()
            q2[h][s].start()
            q3_copy(h, s, c, 0).start()

    def q2_forward(h):
        for s in range(2):
            q2[h][s].forward_left()
            q3_copy(h, s, c, 1).start()
            q2[h][s].forward_right()
            q3_copy(h, s, c, 2).start()

    def q2_finish(h):
        for s in range(2):
            q2[h][s].finish()
            q3_copy(h, s, c, 3).start()

    def q3_wait(h):
        for s in range(2):
            for n in range(4):
                q3_copy(h, s, oc, n).wait_recv()

    def attend_new():
        causal = lax.broadcasted_iota(jnp.int32, (QROWS, ROWS), 1) <= (
            lax.broadcasted_iota(jnp.int32, (QROWS, ROWS), 0) & (ROWS - 1)
        )
        ones = jnp.ones((ROWS, HD), BF16)
        for h in range(2):
            key = normed_rope(ACC[:, 1024 + h * HD : 1024 + (h + 1) * HD], k_gain[...], cos_new, sin_new)
            val = ACC[:, 1280 + h * HD : 1280 + (h + 1) * HD].astype(BF16)
            query = jnp.concatenate([QS[h][0, q_at[0]], QS[h][1, q_at[1]]], axis=0)
            scores = nt(query, key) * SCALE
            weights = jnp.where(causal, jnp.exp(scores), 0.0).astype(BF16)
            NEWCTX[h] = nn(weights, jnp.concatenate([val, ones], axis=1))

    first_dev = ((xup, xdn), (yup, ydn))
    last_dev = ((yup, ydn), (xup, xdn))
    first_at, last_at = (x, y), (y, x)

    def mine(h, s, o, b, core):
        a = rot(first_at[s], o)
        chip = b * 4 + a if s == 0 else a * 4 + b
        return CTX[h, TS[0, chip * 2 + core], s]

    def value(h, s, o, b):
        return mine(h, s, o, b, c).astype(F32) + R0[h, s, o, b].astype(F32)

    def c0_copy(h, s, o):
        return rcopy(S0.at[s, o], R0.at[h, s, o], c0s.at[h, s, o], c0r.at[h, s, o], sib)

    def c0(h):
        for o in (2, 1, 3, 0):
            for s in range(2):

                def fill(b, carry):
                    S0[s, o, b] = mine(h, s, o, b, oc)
                    return carry

                lax.fori_loop(0, 4, fill, 0)
                c0_copy(h, s, o).start()

    def c1o_copy(h, s, d):
        part = pl.ds(d * 2, 2)
        return rcopy(S1O.at[h, s, part], R1O.at[h, s, part], c1os.at[h, s, d], c1or.at[h, s, d], first_dev[s][d])

    def c1m_copy(h, s, d, n):
        part = pl.ds(n * 2, 2)
        return rcopy(
            S1M.at[h, s, d, part], R1M.at[h, s, d, part], c1ms.at[h, s, d, n], c1mr.at[h, s, d, n], first_dev[s][d]
        )

    cuts = (pl.ds(0, 128), pl.ds(128, HALF - 128))

    def c2o_copy(h, s, d):
        return rcopy(
            S2O.at[h, s, cuts[d]], R2O.at[h, s, cuts[d]], c2os.at[h, s, d], c2or.at[h, s, d], last_dev[s][d]
        )

    def c2m_copy(h, s, d, n):
        return rcopy(
            S2M.at[h, s, d, cuts[n]], R2M.at[h, s, d, cuts[n]], c2ms.at[h, s, d, n], c2mr.at[h, s, d, n], last_dev[s][d]
        )

    def c1(h):
        for s in range(2):
            c0_copy(h, s, 2).wait_recv()

            def fill(b, carry):
                S1O[h, s, b] = value(h, s, 2, b).astype(BF16)
                return carry

            lax.fori_loop(0, 4, fill, 0)
            for d in range(2):
                c1o_copy(h, s, d).start()
        for d in range(2):
            for s in range(2):
                o, n = (1, 3)[d], 1 - d
                c0_copy(h, s, o).wait_recv()

                def fill(b, carry):
                    S1M[h, s, d, b] = value(h, s, o, b).astype(BF16)
                    return carry

                lax.fori_loop(n * 2, n * 2 + 2, fill, 0)
                c1m_copy(h, s, d, n).start()

    def c2(h):
        for d in range(2):
            for s in range(2):
                o = (1, 3)[d]
                c1o_copy(h, s, d).wait_recv()

                def fill(b, carry):
                    S1M[h, s, d, b] = (value(h, s, o, b) + R1O[h, s, b].astype(F32)).astype(BF16)
                    return carry

                lax.fori_loop(d * 2, d * 2 + 2, fill, 0)
                c1m_copy(h, s, d, d).start()

    def c3(h):
        for s in range(2):
            c0_copy(h, s, 0).wait_recv()
            for d in range(2):
                for n in range(2):
                    c1m_copy(h, s, d, n).wait_recv()

            def fill(b, carry):
                A1[s, b] = value(h, s, 0, b) + R1M[h, s, 0, b].astype(F32) + R1M[h, s, 1, b].astype(F32)
                return carry

            lax.fori_loop(0, 4, fill, 0)
            S2O[h, s] = A1[s, rot(last_at[s], 2)].astype(BF16)
            for d in range(2):
                c2o_copy(h, s, d).start()
            for d in range(2):
                n = 1 - d
                S2M[h, s, d, cuts[n], :] = A1[s, rot(last_at[s], (1, 3)[d]), cuts[n], :].astype(BF16)
                c2m_copy(h, s, d, n).start()

    def c4(h):
        for s in range(2):
            for d in range(2):
                c2o_copy(h, s, d).wait_recv()
                relayed = A1[s, rot(last_at[s], (1, 3)[d]), cuts[d], :] + R2O[h, s, cuts[d], :].astype(F32)
                S2M[h, s, d, cuts[d], :] = relayed.astype(BF16)
                c2m_copy(h, s, d, d).start()

    def c5(h):
        for s in range(2):
            for d in range(2):
                for n in range(2):
                    c2m_copy(h, s, d, n).wait_recv()
            FIN[...] = A1[s, last_at[s]] + R2M[h, s, 0].astype(F32) + R2M[h, s, 1].astype(F32)
            for g in range(2):
                n = s * 2 + g
                mixed = FIN[g * ROWS : (g + 1) * ROWS, :] + NEWCTX[h, n * ROWS : (n + 1) * ROWS, :HD]
                sums = jnp.sum(jnp.where(eye, FIN[256 + g : 257 + g, :], 0.0), axis=1, keepdims=True)
                sums = sums + NEWCTX[h, n * ROWS : (n + 1) * ROWS, HD:]
                m = h * GROUP + n
                out[:, m * HD : (m + 1) * HD] = (mixed / sums).astype(BF16)

    def step(i, carry):
        def at_step(k):
            return pl.when(i == k)

        @pl.when(i < ITEMS - 2)
        def _():
            opposite(i + 2)

        @pl.when(i < ITEMS)
        def _():
            neighbours(i)

        @at_step(0)
        def _():
            q1_forward(0)

        @at_step(2)
        def _():
            q2_forward(0)
            q2_start(1)

        @pl.when(i >= 1)
        def _():
            own(i - 1)

        @at_step(0)
        def _():
            q2_start(0)

        @at_step(1)
        def _():
            q1_forward(1)

        @at_step(3)
        def _():
            q2_finish(0)
            w_wait(1)

        @at_step(4)
        def _():
            q2_forward(1)
            attend_new()

        @at_step(5)
        def _():
            q3_wait(0)
            attend_pages(0, 0, 6)

        @at_step(6)
        def _():
            attend_pages(0, 6, PAGES)
            c0(0)
            q2_finish(1)

        @at_step(7)
        def _():
            c1(0)

        @at_step(8)
        def _():
            q3_wait(1)
            attend_pages(1, 0, 4)
            c2(0)

        @pl.when(i >= 9)
        def _():
            attend_pages(1, 2 * (i - 7), 2 * (i - 6))

        for k, stage in ((9, c3), (10, c4), (11, c5)):

            @at_step(k)
            def _(stage=stage):
                stage(0)

        return carry

    lax.fori_loop(0, ITEMS + 1, step, 0)
    for o in range(4):
        for s in range(2):
            c0_copy(0, s, o).wait_send()
    for stage in (c0, c1, c2, c3, c4, c5):
        stage(1)

    for kv in range(2):
        for h in range(2):
            for e in (1, 2, 3):
                w1_copy(e, h, kv).wait_send()
            w_rings[h][kv].drain()
            for n in range(4):
                w3_copy(h, kv, c, n).wait_send()
    nh_ring.drain()
    for e in (1, 2, 3):
        rcopy(SSQ.at[z], SSQ.at[z], sqs.at[e], sqr.at[e], zdev[e]).wait_send()

    def drain(i, carry):
        for s in range(2):
            opp_copy(i, s).wait_send()
            mid_copy(i, s).wait_send()
        return carry

    lax.fori_loop(0, ITEMS, drain, 0)
    for o in range(4):
        for s in range(2):
            c0_copy(1, s, o).wait_send()
    for h in range(2):
        for s in range(2):
            q1[h][s].drain()
            q2[h][s].drain()
            for n in range(4):
                q3_copy(h, s, c, n).wait_send()
            for d in range(2):
                c1o_copy(h, s, d).wait_send()
                c2o_copy(h, s, d).wait_send()
                for n in range(2):
                    c1m_copy(h, s, d, n).wait_send()
                    c2m_copy(h, s, d, n).wait_send()


def local(store, new_hidden, wq, wk, wv, norm_gain, q_gain, k_gain, page_table, hist_len):
    tables = [jnp.asarray(t) for t in rope_tables()]
    vm = pl.BlockSpec(memory_space=pltpu.VMEM)
    hbm = pl.BlockSpec(memory_space=pl.ANY)
    dma = pltpu.SemaphoreType.DMA
    scratch = [
        pltpu.VMEM((PAGES, ROWS, FEAT), BF16),
        pltpu.VMEM((4, 2, 2, FEAT, HD), BF16),
        pltpu.VMEM((2, FEAT, 1024), BF16),
        pltpu.VMEM((2, FEAT, 256), BF16),
        pltpu.VMEM((2, FEAT, 256), BF16),
        pltpu.VMEM((ROWS, 1536), F32),
        pltpu.VMEM((4, ROWS, FEAT), BF16),
        pltpu.VMEM((4, 16, ROWS), F32),
        pltpu.VMEM((ROWS, ROWS), F32),
        pltpu.VMEM((ITEMS, 2, ROWS, 256), BF16),
        pltpu.VMEM((ITEMS, 2, ROWS, 256), BF16),
        pltpu.VMEM((ITEMS, 2, 2, ROWS, 256), BF16),
        pltpu.VMEM((ITEMS, 2, 2, ROWS, 256), BF16),
        pltpu.VMEM((2 * PAGES, ROWS, HD), BF16),
        pltpu.VMEM((2 * PAGES, ROWS, 2 * HD), BF16),
        pltpu.VMEM((2, QROWS, 2 * HD), F32),
        pltpu.VMEM((2, REQS, QROWS // 2, HD), BF16),
        pltpu.VMEM((2, REQS, QROWS // 2, HD), BF16),
        pltpu.VMEM((2, PAGES + 1, 2, HALF, HD), BF16),
        pltpu.VMEM((2, 4, 4, HALF, HD), BF16),
        pltpu.VMEM((2, 2, 4, 4, HALF, HD), BF16),
        pltpu.VMEM((2, 2, 4, HALF, HD), BF16),
        pltpu.VMEM((2, 2, 4, HALF, HD), BF16),
        pltpu.VMEM((2, 2, 2, 4, HALF, HD), BF16),
        pltpu.VMEM((2, 2, 2, 4, HALF, HD), BF16),
        pltpu.VMEM((2, 4, HALF, HD), F32),
        pltpu.VMEM((2, 2, HALF, HD), BF16),
        pltpu.VMEM((2, 2, HALF, HD), BF16),
        pltpu.VMEM((2, 2, 2, HALF, HD), BF16),
        pltpu.VMEM((2, 2, 2, HALF, HD), BF16),
        pltpu.VMEM((HALF, HD), F32),
        pltpu.VMEM((24, HD), jnp.int32),
        pltpu.SMEM((24, HD), jnp.int32),
        dma((8,)), dma((2, 3)),
        dma((2, 2, 4)), dma((2, 2, 4)), dma((2, 2, 4)), dma((2, 2, 4)), dma((2, 2, 4)), dma((2, 2, 4)),
        dma((4,)), dma((4,)), dma((4,)), dma((4,)),
        dma((ITEMS, 2)), dma((ITEMS, 2)), dma((ITEMS, 2)), dma((ITEMS, 2)),
        dma((2, 2, 4)), dma((2, 2, 4)), dma((2, 2, 4)), dma((2, 2, 4)), dma((2, 2, 4)), dma((2, 2, 4)),
        dma((2, 2, 4)), dma((2, 2, 4)),
        dma((2, 2, 2)), dma((2, 2, 2)), dma((2, 2, 2, 2)), dma((2, 2, 2, 2)),
        dma((2, 2, 2)), dma((2, 2, 2)), dma((2, 2, 2, 2)), dma((2, 2, 2, 2)),
    ]
    return pl.pallas_call(
        kernel,
        out_shape=jax.ShapeDtypeStruct((ROWS, 2 * GROUP * HD), BF16),
        in_specs=[vm, pl.BlockSpec(memory_space=pltpu.SMEM)] + [hbm] * 5 + [vm] * 7,
        out_specs=vm,
        scratch_shapes=scratch,
        compiler_params=pltpu.CompilerParams(
            collective_id=0, has_side_effects=True, vmem_limit_bytes=63 * 1024 * 1024
        ),
        cost_estimate=pl.CostEstimate(flops=12_000_000_000, bytes_accessed=25_000_000, transcendentals=2_000_000),
    )(
        page_table.T, hist_len, store, new_hidden, wq, wk, wv, norm_gain.reshape(WIDE // HD, HD),
        q_gain.reshape(1, HD), k_gain.reshape(1, HD), *tables,
    )


def solution(mesh):
    return jax.shard_map(
        local,
        mesh=mesh,
        in_specs=(
            P("pool", None, "tensor"),
            P("pool", "tensor"),
            P(None, "tensor"),
            P(None, "tensor"),
            P(None, "tensor"),
            P(),
            P(),
            P(),
            P(),
            P(),
        ),
        out_specs=P("pool", "tensor"),
        check_vma=False,
    )
```

```python
import jax
import jax.numpy as jnp
import numpy as np
from jax import lax
from jax.experimental import pallas as pl
from jax.experimental.pallas import tpu as pltpu
from jax.sharding import PartitionSpec as P

EPS = 1e-06
ROPE_BASE = 1000000.0
MESH = pl.DeviceIdType.MESH
F32 = jnp.float32
BF16 = jnp.bfloat16

PAGES = 12
ROWS = 128
FEAT = 1280
NZ = 4
WIDE = FEAT * NZ
HD = 128
GROUP = 4
QROWS = GROUP * ROWS
REQS = 32
ITEMS = 12
HALF = 272
SEG = 160
SCALE = HD ** -0.5


def rope_tables():
    freq = ROPE_BASE ** (-np.arange(64, dtype=np.float64) * 2.0 / HD)
    freq = np.concatenate([freq, freq])[None, :]
    rows = np.arange(ROWS, dtype=np.float64)[:, None] * freq
    pages = np.arange(24, dtype=np.float64)[:, None] * ROWS * freq
    return [np.asarray(t, np.float32) for t in (np.cos(rows), np.sin(rows), np.cos(pages), np.sin(pages))]


class Ring:
    def __init__(self, piece, half, at, dev_up, dev_down, send, recv):
        self.piece, self.half, self.at = piece, half, at
        self.up, self.down, self.send, self.recv = dev_up, dev_down, send, recv
        self.left = lax.rem(at + 3, 4)
        self.right = lax.rem(at + 1, 4)
        self.opp = lax.rem(at + 2, 4)

    def copy(self, ref, k, dev):
        return pltpu.make_async_remote_copy(
            src_ref=ref, dst_ref=ref, send_sem=self.send(k), recv_sem=self.recv(k), device_id=dev, device_id_type=MESH
        )

    def start(self):
        self.copy(self.piece(self.at), 0, self.up).start()
        self.copy(self.piece(self.at), 1, self.down).start()

    def forward_left(self):
        self.copy(self.piece(self.left), 0, self.up).wait_recv()
        self.copy(self.half(self.left, 0), 2, self.up).start()

    def forward_right(self):
        self.copy(self.piece(self.right), 1, self.down).wait_recv()
        self.copy(self.half(self.right, 1), 3, self.down).start()

    def finish(self):
        self.copy(self.half(self.opp, 0), 2, self.up).wait_recv()
        self.copy(self.half(self.opp, 1), 3, self.down).wait_recv()

    def drain(self):
        self.copy(self.piece(self.at), 0, self.up).wait_send()
        self.copy(self.piece(self.at), 1, self.down).wait_send()
        self.copy(self.half(self.left, 0), 2, self.up).wait_send()
        self.copy(self.half(self.right, 1), 3, self.down).wait_send()


class Spread:
    def __init__(self, piece, at, devs, send, recv):
        self.piece, self.devs, self.send, self.recv = piece, devs, send, recv
        self.places = [lax.rem(at + d, 4) for d in (0, 3, 1, 2)]

    def copy(self, place, n):
        ref = self.piece(place)
        return pltpu.make_async_remote_copy(
            src_ref=ref, dst_ref=ref, send_sem=self.send(n), recv_sem=self.recv(n),
            device_id=self.devs[n], device_id_type=MESH,
        )

    def start(self):
        for n in range(3):
            self.copy(self.places[0], n).start()

    def wait(self, n):
        self.copy(self.places[n + 1], n).wait_recv()

    def drain(self):
        for n in range(3):
            self.copy(self.places[0], n).wait_send()


def nt(a, b):
    return lax.dot_general(a, b, (((1,), (1,)), ((), ())), preferred_element_type=F32)


def nn(a, b):
    return jnp.dot(a, b, preferred_element_type=F32)


def kernel(
    table_in, lengths, store, new_hidden, wq, wk, wv, norm_gain_in, q_gain_in, k_gain_in, cosr_in, sinr_in, cosp_in, sinp_in,
    out,
    X, W, WQB, WKB, WVB, ACC, NH, SSQ, INV, OPPS, OPPR, MIDS, MIDR, KB, VB, NEWCTX, QA, QB, CTX,
    S0, R0, S1O, R1O, S1M, R1M, A1, S2M, R2M, FIN, TV, TS,
    table, norm_gain, q_gain, k_gain, cosr, sinr, cosp, sinp,
    lsem, wbsem, w1s, w1r, w2s, w2r, w3s, w3r, nhs, nhr, sqs, sqr, os_, or_, ms, mr,
    q1s, q1r, q2s, q2r, q3s, q3r, c0s, c0r, c1os, c1or, c1ms, c1mr, c2s, c2r,
):
    QS = (QA, QB)
    p = lax.axis_index("pool")
    z = lax.axis_index("tensor")
    c = lax.rem(p, 2)
    x = lax.rem(p // 2, 4)
    y = p // 8
    oc = 1 - c

    def at(yy, xx, cc):
        return yy * 8 + xx * 2 + cc

    def rot(v, d):
        return lax.rem(v + d, 4)

    zdev = [(p, rot(z, d)) for d in range(4)]
    xup, xdn = (at(y, rot(x, 1), c), z), (at(y, rot(x, 3), c), z)
    yup, ydn = (at(rot(y, 1), x, c), z), (at(rot(y, 3), x, c), z)
    sib = (at(y, x, oc), z)
    xall = (xup, xdn, (at(y, rot(x, 2), c), z))
    yall = (yup, ydn, (at(rot(y, 2), x, c), z))

    def rcopy(src, dst, ss, rs, dev):
        return pltpu.make_async_remote_copy(
            src_ref=src, dst_ref=dst, send_sem=ss, recv_sem=rs, device_id=dev, device_id_type=MESH
        )

    ld_new = pltpu.make_async_copy(new_hidden, NH.at[z], lsem.at[0])
    ld_new.start()
    ld_x = [pltpu.make_async_copy(store.at[pl.ds(6 * n, 6)], X.at[pl.ds(6 * n, 6)], lsem.at[1 + n]) for n in range(2)]
    for cp in ld_x:
        cp.start()

    small = [
        (table_in, table), (norm_gain_in, norm_gain), (q_gain_in, q_gain), (k_gain_in, k_gain),
        (cosr_in, cosr), (sinr_in, sinr), (cosp_in, cosp), (sinp_in, sinp),
    ]
    ld_small = [pltpu.make_async_copy(src, dst, lsem.at[8 + n]) for n, (src, dst) in enumerate(small)]
    for cp in ld_small:
        cp.start()

    barrier = pltpu.get_barrier_semaphore()
    peers = [*zdev[1:], *xall, *yall, sib]
    for dev in peers:
        pl.semaphore_signal(barrier, inc=1, device_id=dev, device_id_type=MESH)

    def block_loads(d):
        rows = pl.ds(pl.multiple_of(rot(z, d) * FEAT, FEAT), FEAT)
        b = (0, 1, 1, 0)[d]
        return [
            pltpu.make_async_copy(wq.at[rows, :], WQB.at[b], wbsem.at[b, 0]),
            pltpu.make_async_copy(wk.at[rows, :], WKB.at[b], wbsem.at[b, 1]),
            pltpu.make_async_copy(wv.at[rows, :], WVB.at[b], wbsem.at[b, 2]),
        ]

    own_rows = pl.ds(pl.multiple_of(z * FEAT, FEAT), FEAT)
    ld_w = []
    for h in range(2):
        for kv, ref in enumerate((wk, wv)):
            ld_w.append(
                pltpu.make_async_copy(
                    ref.at[own_rows, h * HD : (h + 1) * HD], W.at[0, h, kv], lsem.at[4 + 2 * h + kv]
                )
            )

    pl.semaphore_wait(barrier, len(peers))
    ring_at = (x, y)

    def seg_rows(cc, k):
        return pl.ds(pl.multiple_of(cc * (4 * SEG) + k * SEG, SEG), SEG)

    def w1_copy(e, h, kv):
        ref = (wk, wv)[kv]
        seg = pl.multiple_of(c * (4 * SEG) + ring_at[kv] * SEG, SEG)
        src = ref.at[pl.ds(pl.multiple_of(rot(z, e) * FEAT + seg, SEG), SEG), h * HD : (h + 1) * HD]
        return rcopy(src, W.at[4 - e, h, kv, pl.ds(seg, SEG), :], w1s.at[kv, h, e], w1r.at[kv, h, 4 - e], zdev[e])

    nh_ring = Ring(
        lambda k: NH.at[k], lambda k, s: NH.at[k, pl.ds(64 * s, 64), :], z, zdev[1], zdev[3],
        lambda k: nhs.at[k], lambda k: nhr.at[k],
    )
    def w1_start(h):
        for kv in range(2):
            for e in (2, 1, 3):
                w1_copy(e, h, kv).start()

    w1_start(0)

    def w1_wait(slot, h, kv):
        seg = pl.multiple_of(c * (4 * SEG) + ring_at[kv] * SEG, SEG)
        dst = W.at[slot, h, kv, pl.ds(seg, SEG), :]
        rcopy(dst, dst, w1s.at[kv, h, slot], w1r.at[kv, h, slot], zdev[slot]).wait_recv()

    for cp in ld_small:
        cp.wait()
    page = table[...] - p * PAGES
    hit = jnp.logical_and(page >= 0, page < PAGES)
    rank = lax.broadcasted_iota(jnp.int32, (16, REQS), 0)
    slots = PAGES + jnp.sum(jnp.where(hit, page - PAGES, 0), axis=0, keepdims=True)
    askers = jnp.where(slots == rank, lax.broadcasted_iota(jnp.int32, (16, REQS), 1), 0)
    TV[...] = jnp.zeros_like(TV)
    TV[0:1, :REQS] = jnp.clip(slots, 0, PAGES)
    TV[1:2, :REQS] = jnp.clip(jnp.sum(jnp.where(hit, rank, 0), axis=0, keepdims=True), 0, 15)
    TV[8:24, :] = jnp.broadcast_to(jnp.clip(jnp.sum(askers, axis=1, keepdims=True), 0, REQS - 1), (16, HD))
    to_scalar = pltpu.make_async_copy(TV, TS, lsem.at[3])
    to_scalar.start()

    CTX[0, PAGES] = jnp.zeros((2, HALF, HD), BF16)
    CTX[1, PAGES] = jnp.zeros((2, HALF, HD), BF16)

    lane = lax.broadcasted_iota(jnp.int32, (ROWS, ROWS), 1)
    row = lax.broadcasted_iota(jnp.int32, (ROWS, ROWS), 0)
    eye = lane == row

    def gain_of(zz):
        return jnp.concatenate([norm_gain[pl.ds(zz * (FEAT // HD) + k, 1), :] for k in range(FEAT // HD)], axis=1)


    def squares_of(v):
        v = v.astype(F32)
        return jnp.sum(v * v, axis=1, keepdims=True)

    ld_new.wait()
    squares = jnp.where(lane == PAGES, squares_of(NH[z]), 0.0)
    for n in range(2):
        ld_x[n].wait()
        squares = lax.fori_loop(
            6 * n, 6 * n + 6, lambda j, acc: jnp.where(lane == j, squares_of(X[j]), acc), squares
        )
    SSQ[z] = jnp.transpose(squares)[:16, :]
    for e in (1, 2, 3):
        rcopy(SSQ.at[z], SSQ.at[z], sqs.at[e], sqr.at[e], zdev[e]).start()
    nh_ring.start()
    w1_start(1)
    to_scalar.wait()

    for d in (0, 1):
        for cp in block_loads(d):
            cp.start()
    for cp in ld_w:
        cp.start()

    def normed(v, j, gain):
        inv = jnp.sum(jnp.where(lane == j, INV[...], 0.0), axis=1, keepdims=True)
        return (v.astype(F32) * inv * gain).astype(BF16)

    def prepare(j, carry):
        X[j] = normed(X[j], j, gain)
        return carry

    def w_piece(h, kv, cc):
        return lambda k: W.at[pl.ds(1, 3), h, kv, seg_rows(cc, k), :]

    def w_spread_of(h, kv):
        return Spread(
            w_piece(h, kv, c), ring_at[kv], (xall, yall)[kv], lambda n: w2s.at[h, kv, n], lambda n: w2r.at[h, kv, n]
        )

    w_spread = [[w_spread_of(h, kv) for kv in range(2)] for h in range(2)]

    def w3_copy(h, kv, cc, n):
        ref = w_piece(h, kv, cc)(w_spread[h][kv].places[n])
        return rcopy(ref, ref, w3s.at[h, kv, n], w3r.at[h, kv, n], sib)

    def w_start(h):
        for kv in range(2):
            for slot in (1, 2, 3):
                w1_wait(slot, h, kv)
            w_spread[h][kv].start()
            w3_copy(h, kv, c, 0).start()

    def w_share(h):
        for n in range(3):
            for kv in range(2):
                w_spread[h][kv].wait(n)
                w3_copy(h, kv, c, n + 1).start()

    def w_wait(h):
        for kv in range(2):
            for n in range(4):
                w3_copy(h, kv, oc, n).wait_recv()
            ld_w[2 * h + kv].wait()

    sign = jnp.where(lax.broadcasted_iota(jnp.int32, (1, HD), 1) < HD // 2, -1.0, 1.0).astype(F32)
    cos_r, sin_r = cosr[...], sinr[...]

    def angle_at(first_cos, first_sin):
        return first_cos * cos_r - first_sin * sin_r, (first_sin * cos_r + first_cos * sin_r) * sign

    def normed_rope(v, g, cos, sin):
        v = v * lax.rsqrt(jnp.mean(v * v, axis=1, keepdims=True) + EPS) * g
        return (v * cos + pltpu.roll(v, HD // 2, 1) * sin).astype(BF16)

    def project_new(d):
        for cp in block_loads(d):
            cp.wait()
        b = (0, 1, 1, 0)[d]
        a = normed(NH[rot(z, d)], PAGES, gain_of(rot(z, d)))
        parts = ((0, WQB), (1024, WKB), (1280, WVB))
        for first, ref in parts:
            width = ref.shape[2]
            prod = nn(a, ref[b])
            if d == 0:
                ACC[:, first : first + width] = prod
            else:
                ACC[:, first : first + width] += prod
        if d < 2:
            for cp in block_loads(3 - d):
                cp.start()

    w_start(0)
    for e in (1, 2, 3):
        far = SSQ.at[rot(z, 4 - e)]
        rcopy(far, far, sqs.at[e], sqr.at[e], zdev[e]).wait_recv()
    total = SSQ[0] + SSQ[1] + SSQ[2] + SSQ[3]
    inverse = lax.rsqrt(total * (1.0 / WIDE) + EPS)
    INV[...] = jnp.transpose(jnp.concatenate([inverse, jnp.zeros((ROWS - 16, ROWS), F32)], axis=0))

    gain = gain_of(z)
    lax.fori_loop(0, PAGES, prepare, 0)
    project_new(0)
    nh_ring.forward_left()
    nh_ring.forward_right()
    w_share(0)
    w_wait(0)

    def product(i, slot):
        h, pair = i // 6, lax.rem(i, 6)
        a = X[pl.ds(pair * 2, 2)].reshape(2 * ROWS, FEAT)
        return nn(a, jnp.concatenate([W[slot, h, 0], W[slot, h, 1]], axis=1))

    def opp_copy(i, s):
        return rcopy(OPPS.at[i, s], OPPR.at[i, s], os_.at[i, s], or_.at[i, s], (zdev[1], zdev[3])[s])

    def mid_copy(i, s):
        return rcopy(MIDS.at[i, s], MIDR.at[i, s], ms.at[i, s], mr.at[i, s], (zdev[1], zdev[3])[s])

    def opposite(i):
        part = product(i, 2).astype(BF16)
        for s in range(2):
            OPPS[i, s] = part[s * ROWS : (s + 1) * ROWS]
            opp_copy(i, s).start()

    def neighbours(i):
        for s in range(2):
            part = product(i, (1, 3)[s])
            opp_copy(i, s).wait_recv()
            for t in range(2):
                page = part[t * ROWS : (t + 1) * ROWS]
                if t == s:
                    page = page + OPPR[i, s].astype(F32)
                MIDS[i, s, t] = page.astype(BF16)
            mid_copy(i, s).start()

    def own(i):
        h, pair = i // 6, lax.rem(i, 6)
        part = product(i, 0)
        for s in range(2):
            mid_copy(i, s).wait_recv()
        for t in range(2):
            j = pair * 2 + t
            page = part[t * ROWS : (t + 1) * ROWS] + MIDR[i, 0, t].astype(F32) + MIDR[i, 1, t].astype(F32)
            n = h * PAGES + j
            request = TS[8 + j, 0]
            i_page = TS[1, request]
            cos, sin = angle_at(cosp[pl.ds(i_page, 1), :], sinp[pl.ds(i_page, 1), :])
            KB[n] = normed_rope(page[:, :HD], k_gain[...], cos, sin)
            live = row < lengths[request] - i_page * ROWS
            VB[n, :, :HD] = jnp.where(live, page[:, HD:], 0.0).astype(BF16)
            VB[n, :, HD:] = jnp.where(live, 1.0, 0.0).astype(BF16)

    def attend(h, j):
        n = h * PAGES + j
        request = TS[8 + j, 0]
        core, xx, yy = lax.rem(request, 2), lax.rem(request // 2, 4), request // 8
        query = jnp.concatenate(
            [QS[h][0, core * 16 + yy * 4 + xx], QS[h][1, core * 16 + xx * 4 + yy]], axis=0
        )
        scores = nt(query, KB[n]) * SCALE
        mixed = nn(jnp.exp(scores).astype(BF16), VB[n])
        line = lax.broadcasted_iota(jnp.int32, (16, HD), 0)
        for s in range(2):
            CTX[h, j, s, :256, :] = mixed[s * 256 : (s + 1) * 256, :HD].astype(BF16)
            sums = []
            for g in range(2):
                block = mixed[s * 256 + g * ROWS : s * 256 + (g + 1) * ROWS, HD:]
                sums.append(jnp.sum(jnp.where(eye, block, 0.0), axis=0, keepdims=True))
            CTX[h, j, s, 256:, :] = jnp.where(line == 0, sums[0], jnp.where(line == 1, sums[1], 0.0)).astype(BF16)

    def attend_pages(h, first, last):
        def one(j, carry):
            attend(h, j)
            return carry

        lax.fori_loop(first, last, one, 0)

    q_at = (c * 16 + y * 4 + x, c * 16 + x * 4 + y)

    def q1_of(h, s):
        base = c * 16 + (y * 4, x * 4)[s]
        return Spread(
            lambda k: QS[h].at[s, base + k], (x, y)[s], (xall, yall)[s], lambda n: q1s.at[h, s, n], lambda n: q1r.at[h, s, n]
        )

    def q2_of(h, s):
        return Spread(
            lambda k: QS[h].at[s, pl.ds(c * 16 + k * 4, 4)], (y, x)[s], (yall, xall)[s],
            lambda n: q2s.at[h, s, n], lambda n: q2r.at[h, s, n],
        )

    q1 = [[q1_of(h, s) for s in range(2)] for h in range(2)]
    q2 = [[q2_of(h, s) for s in range(2)] for h in range(2)]

    def q3_copy(h, s, cc, n):
        ref = QS[h].at[s, pl.ds(cc * 16 + q2[h][s].places[n] * 4, 4)]
        return rcopy(ref, ref, q3s.at[h, s, n], q3r.at[h, s, n], sib)

    def angles_new():
        length = lengths[p]
        page_cos, page_sin = cosp[pl.ds(length // ROWS, 1), :], sinp[pl.ds(length // ROWS, 1), :]
        rest_cos, rest_sin = cosr[pl.ds(lax.rem(length, ROWS), 1), :], sinr[pl.ds(lax.rem(length, ROWS), 1), :]
        return angle_at(page_cos * rest_cos - page_sin * rest_sin, page_sin * rest_cos + page_cos * rest_sin)

    def q_begin():
        nh_ring.finish()
        project_new(2)
        cos_new, sin_new = angles_new()
        for h in range(2):
            for s in range(2):
                for g in range(2):
                    n = h * GROUP + s * 2 + g
                    raw = ACC[:, n * HD : (n + 1) * HD]
                    QS[h][s, q_at[s], g * ROWS : (g + 1) * ROWS, :] = normed_rope(raw, q_gain[...], cos_new, sin_new)
                q1[h][s].start()

    def q_along(h):
        for s in range(2):
            for n in range(3):
                q1[h][s].wait(n)
            q2[h][s].start()
            q3_copy(h, s, c, 0).start()

    def q_share(h):
        for n in range(3):
            for s in range(2):
                q2[h][s].wait(n)
                q3_copy(h, s, c, n + 1).start()

    def q_wait(h):
        for s in range(2):
            for n in range(4):
                q3_copy(h, s, oc, n).wait_recv()

    def attend_new():
        cos_new, sin_new = angles_new()
        causal = lax.broadcasted_iota(jnp.int32, (QROWS, ROWS), 1) <= (
            lax.broadcasted_iota(jnp.int32, (QROWS, ROWS), 0) & (ROWS - 1)
        )
        ones = jnp.ones((ROWS, HD), BF16)
        for h in range(2):
            key = normed_rope(ACC[:, 1024 + h * HD : 1024 + (h + 1) * HD], k_gain[...], cos_new, sin_new)
            val = ACC[:, 1280 + h * HD : 1280 + (h + 1) * HD].astype(BF16)
            query = jnp.concatenate([QS[h][0, q_at[0]], QS[h][1, q_at[1]]], axis=0)
            scores = nt(query, key) * SCALE
            weights = jnp.where(causal, jnp.exp(scores), 0.0).astype(BF16)
            NEWCTX[h] = nn(weights, jnp.concatenate([val, ones], axis=1))

    first_dev = ((xup, xdn), (yup, ydn))
    last_dev = (yall, xall)
    first_at, last_at = (x, y), (y, x)

    def mine(h, s, o, b, core):
        a = rot(first_at[s], o)
        chip = b * 4 + a if s == 0 else a * 4 + b
        return CTX[h, TS[0, chip * 2 + core], s]

    def value(h, s, o, b):
        return mine(h, s, o, b, c).astype(F32) + R0[h, s, o, b].astype(F32)

    def c0_copy(h, s, o):
        return rcopy(S0.at[s, o], R0.at[h, s, o], c0s.at[h, s, o], c0r.at[h, s, o], sib)

    def c0(h):
        for o in (2, 1, 3, 0):
            for s in range(2):

                def fill(b, carry):
                    S0[s, o, b] = mine(h, s, o, b, oc)
                    return carry

                lax.fori_loop(0, 4, fill, 0)
                c0_copy(h, s, o).start()

    def c1o_copy(h, s, d):
        part = pl.ds(d * 2, 2)
        return rcopy(S1O.at[h, s, part], R1O.at[h, s, part], c1os.at[h, s, d], c1or.at[h, s, d], first_dev[s][d])

    def c1m_copy(h, s, d, n):
        part = pl.ds(n * 2, 2)
        return rcopy(
            S1M.at[h, s, d, part], R1M.at[h, s, d, part], c1ms.at[h, s, d, n], c1mr.at[h, s, d, n], first_dev[s][d]
        )

    def c2_copy(h, s, n):
        return rcopy(S2M.at[h, s, n], R2M.at[h, s, n], c2s.at[h, s, n], c2r.at[h, s, n], last_dev[s][n])

    def c1(h):
        for s in range(2):
            c0_copy(h, s, 2).wait_recv()

            def fill(b, carry):
                S1O[h, s, b] = value(h, s, 2, b).astype(BF16)
                return carry

            lax.fori_loop(0, 4, fill, 0)
            for d in range(2):
                c1o_copy(h, s, d).start()
        for d in range(2):
            for s in range(2):
                o, n = (1, 3)[d], 1 - d
                c0_copy(h, s, o).wait_recv()

                def fill(b, carry):
                    S1M[h, s, d, b] = value(h, s, o, b).astype(BF16)
                    return carry

                lax.fori_loop(n * 2, n * 2 + 2, fill, 0)
                c1m_copy(h, s, d, n).start()

    def c2(h):
        for d in range(2):
            for s in range(2):
                o = (1, 3)[d]
                c1o_copy(h, s, d).wait_recv()

                def fill(b, carry):
                    S1M[h, s, d, b] = (value(h, s, o, b) + R1O[h, s, b].astype(F32)).astype(BF16)
                    return carry

                lax.fori_loop(d * 2, d * 2 + 2, fill, 0)
                c1m_copy(h, s, d, d).start()

    def c3(h):
        for s in range(2):
            c0_copy(h, s, 0).wait_recv()
            for d in range(2):
                for n in range(2):
                    c1m_copy(h, s, d, n).wait_recv()

            def fill(b, carry):
                A1[s, b] = value(h, s, 0, b) + R1M[h, s, 0, b].astype(F32) + R1M[h, s, 1, b].astype(F32)
                return carry

            lax.fori_loop(0, 4, fill, 0)
            for n, o in ((2, 2), (0, 1), (1, 3)):
                S2M[h, s, n] = A1[s, rot(last_at[s], o)].astype(BF16)
                c2_copy(h, s, n).start()

    def c4(h):
        for s in range(2):
            for n in range(3):
                c2_copy(h, s, n).wait_recv()
            parts = R2M[h, s, 0].astype(F32) + R2M[h, s, 1].astype(F32) + R2M[h, s, 2].astype(F32)
            FIN[...] = A1[s, last_at[s]] + parts
            for g in range(2):
                n = s * 2 + g
                mixed = FIN[g * ROWS : (g + 1) * ROWS, :] + NEWCTX[h, n * ROWS : (n + 1) * ROWS, :HD]
                sums = jnp.sum(jnp.where(eye, FIN[256 + g : 257 + g, :], 0.0), axis=1, keepdims=True)
                sums = sums + NEWCTX[h, n * ROWS : (n + 1) * ROWS, HD:]
                m = h * GROUP + n
                out[:, m * HD : (m + 1) * HD] = (mixed / sums).astype(BF16)

    opposite(0)
    opposite(1)
    w_start(1)
    project_new(1)
    project_new(3)

    def step(i, carry):
        def at_step(k, *actions):
            @pl.when(i == k)
            def _():
                for action in actions:
                    action()

        @pl.when(i < ITEMS - 2)
        def _():
            opposite(i + 2)

        @pl.when(i < ITEMS)
        def _():
            neighbours(i)

        @pl.when(i >= 2)
        def _():
            own(i - 2)

        def pages(h, first, last):
            return lambda: attend_pages(h, first, last)

        def of(stage, h):
            return lambda: stage(h)

        at_step(0, q_begin)
        at_step(1, of(w_share, 1))
        at_step(2, of(q_along, 0))
        at_step(3, of(w_wait, 1), attend_new)
        at_step(4, of(q_along, 1))
        at_step(5, of(q_share, 0))
        at_step(6, of(q_wait, 0), pages(0, 0, 4))
        at_step(7, pages(0, 4, 8))
        at_step(8, pages(0, 8, 12), of(c0, 0), of(q_share, 1))
        at_step(9, of(c1, 0), of(q_wait, 1), pages(1, 0, 2))
        at_step(10, pages(1, 2, 5))
        at_step(11, of(c2, 0), pages(1, 5, 8))
        at_step(12, pages(1, 8, 10))
        at_step(13, pages(1, 10, 12))
        return carry

    lax.fori_loop(0, ITEMS + 2, step, 0)
    for o in range(4):
        for s in range(2):
            c0_copy(0, s, o).wait_send()
    c0(1)
    c3(0)
    c1(1)
    c2(1)
    c4(0)
    c3(1)
    c4(1)

    for kv in range(2):
        for h in range(2):
            for e in (1, 2, 3):
                w1_copy(e, h, kv).wait_send()
            w_spread[h][kv].drain()
            for n in range(4):
                w3_copy(h, kv, c, n).wait_send()
    nh_ring.drain()
    for e in (1, 2, 3):
        rcopy(SSQ.at[z], SSQ.at[z], sqs.at[e], sqr.at[e], zdev[e]).wait_send()

    def drain(i, carry):
        for s in range(2):
            opp_copy(i, s).wait_send()
            mid_copy(i, s).wait_send()
        return carry

    lax.fori_loop(0, ITEMS, drain, 0)
    for o in range(4):
        for s in range(2):
            c0_copy(1, s, o).wait_send()
    for h in range(2):
        for s in range(2):
            q1[h][s].drain()
            q2[h][s].drain()
            for n in range(4):
                q3_copy(h, s, c, n).wait_send()
            for d in range(2):
                c1o_copy(h, s, d).wait_send()
                for n in range(2):
                    c1m_copy(h, s, d, n).wait_send()
            for n in range(3):
                c2_copy(h, s, n).wait_send()


def local(store, new_hidden, wq, wk, wv, norm_gain, q_gain, k_gain, page_table, hist_len):
    tables = [jnp.asarray(t) for t in rope_tables()]
    vm = pl.BlockSpec(memory_space=pltpu.VMEM)
    hbm = pl.BlockSpec(memory_space=pl.ANY)
    dma = pltpu.SemaphoreType.DMA
    scratch = [
        pltpu.VMEM((PAGES, ROWS, FEAT), BF16),
        pltpu.VMEM((4, 2, 2, FEAT, HD), BF16),
        pltpu.VMEM((2, FEAT, 1024), BF16),
        pltpu.VMEM((2, FEAT, 256), BF16),
        pltpu.VMEM((2, FEAT, 256), BF16),
        pltpu.VMEM((ROWS, 1536), F32),
        pltpu.VMEM((4, ROWS, FEAT), BF16),
        pltpu.VMEM((4, 16, ROWS), F32),
        pltpu.VMEM((ROWS, ROWS), F32),
        pltpu.VMEM((ITEMS, 2, ROWS, 256), BF16),
        pltpu.VMEM((ITEMS, 2, ROWS, 256), BF16),
        pltpu.VMEM((ITEMS, 2, 2, ROWS, 256), BF16),
        pltpu.VMEM((ITEMS, 2, 2, ROWS, 256), BF16),
        pltpu.VMEM((2 * PAGES, ROWS, HD), BF16),
        pltpu.VMEM((2 * PAGES, ROWS, 2 * HD), BF16),
        pltpu.VMEM((2, QROWS, 2 * HD), F32),
        pltpu.VMEM((2, REQS, QROWS // 2, HD), BF16),
        pltpu.VMEM((2, REQS, QROWS // 2, HD), BF16),
        pltpu.VMEM((2, PAGES + 1, 2, HALF, HD), BF16),
        pltpu.VMEM((2, 4, 4, HALF, HD), BF16),
        pltpu.VMEM((2, 2, 4, 4, HALF, HD), BF16),
        pltpu.VMEM((2, 2, 4, HALF, HD), BF16),
        pltpu.VMEM((2, 2, 4, HALF, HD), BF16),
        pltpu.VMEM((2, 2, 2, 4, HALF, HD), BF16),
        pltpu.VMEM((2, 2, 2, 4, HALF, HD), BF16),
        pltpu.VMEM((2, 4, HALF, HD), F32),
        pltpu.VMEM((2, 2, 3, HALF, HD), BF16),
        pltpu.VMEM((2, 2, 3, HALF, HD), BF16),
        pltpu.VMEM((HALF, HD), F32),
        pltpu.VMEM((24, HD), jnp.int32),
        pltpu.SMEM((24, HD), jnp.int32),
        pltpu.VMEM((16, REQS), jnp.int32),
        pltpu.VMEM((WIDE // HD, HD), F32),
        pltpu.VMEM((1, HD), F32),
        pltpu.VMEM((1, HD), F32),
        pltpu.VMEM((ROWS, HD), F32),
        pltpu.VMEM((ROWS, HD), F32),
        pltpu.VMEM((24, HD), F32),
        pltpu.VMEM((24, HD), F32),
        dma((16,)), dma((2, 3)),
        dma((2, 2, 4)), dma((2, 2, 4)), dma((2, 2, 4)), dma((2, 2, 4)), dma((2, 2, 4)), dma((2, 2, 4)),
        dma((4,)), dma((4,)), dma((4,)), dma((4,)),
        dma((ITEMS, 2)), dma((ITEMS, 2)), dma((ITEMS, 2)), dma((ITEMS, 2)),
        dma((2, 2, 4)), dma((2, 2, 4)), dma((2, 2, 4)), dma((2, 2, 4)), dma((2, 2, 4)), dma((2, 2, 4)),
        dma((2, 2, 4)), dma((2, 2, 4)),
        dma((2, 2, 2)), dma((2, 2, 2)), dma((2, 2, 2, 2)), dma((2, 2, 2, 2)),
        dma((2, 2, 3)), dma((2, 2, 3)),
    ]
    return pl.pallas_call(
        kernel,
        out_shape=jax.ShapeDtypeStruct((ROWS, 2 * GROUP * HD), BF16),
        in_specs=[hbm, pl.BlockSpec(memory_space=pltpu.SMEM)] + [hbm] * 12,
        out_specs=vm,
        scratch_shapes=scratch,
        compiler_params=pltpu.CompilerParams(
            collective_id=0, has_side_effects=True, vmem_limit_bytes=63 * 1024 * 1024
        ),
        cost_estimate=pl.CostEstimate(flops=12_000_000_000, bytes_accessed=25_000_000, transcendentals=2_000_000),
    )(
        page_table.T, hist_len, store, new_hidden, wq, wk, wv, norm_gain.reshape(WIDE // HD, HD),
        q_gain.reshape(1, HD), k_gain.reshape(1, HD), *tables,
    )


def solution(mesh):
    return jax.shard_map(
        local,
        mesh=mesh,
        in_specs=(
            P("pool", None, "tensor"),
            P("pool", "tensor"),
            P(None, "tensor"),
            P(None, "tensor"),
            P(None, "tensor"),
            P(),
            P(),
            P(),
            P(),
            P(),
        ),
        out_specs=P("pool", "tensor"),
        check_vma=False,
    )
```

```python
import jax
import jax.numpy as jnp
import numpy as np
from jax import lax
from jax.experimental import pallas as pl
from jax.experimental.pallas import tpu as pltpu
from jax.sharding import PartitionSpec as P

EPS = 1e-06
ROPE_BASE = 1000000.0
MESH = pl.DeviceIdType.MESH
F32 = jnp.float32
BF16 = jnp.bfloat16

PAGES = 12
ROWS = 128
FEAT = 1280
NZ = 4
WIDE = FEAT * NZ
HD = 128
GROUP = 4
QROWS = GROUP * ROWS
REQS = 32
ITEMS = 12
HALF = 272
SEG = 160
SCALE = HD ** -0.5


def rope_tables():
    freq = ROPE_BASE ** (-np.arange(64, dtype=np.float64) * 2.0 / HD)
    freq = np.concatenate([freq, freq])[None, :]
    rows = np.arange(ROWS, dtype=np.float64)[:, None] * freq
    pages = np.arange(24, dtype=np.float64)[:, None] * ROWS * freq
    return [np.asarray(t, np.float32) for t in (np.cos(rows), np.sin(rows), np.cos(pages), np.sin(pages))]


class Ring:
    def __init__(self, piece, half, at, dev_up, dev_down, send, recv):
        self.piece, self.half, self.at = piece, half, at
        self.up, self.down, self.send, self.recv = dev_up, dev_down, send, recv
        self.left = lax.rem(at + 3, 4)
        self.right = lax.rem(at + 1, 4)
        self.opp = lax.rem(at + 2, 4)

    def copy(self, ref, k, dev):
        return pltpu.make_async_remote_copy(
            src_ref=ref, dst_ref=ref, send_sem=self.send(k), recv_sem=self.recv(k), device_id=dev, device_id_type=MESH
        )

    def start(self):
        self.copy(self.piece(self.at), 0, self.up).start()
        self.copy(self.piece(self.at), 1, self.down).start()

    def forward_left(self):
        self.copy(self.piece(self.left), 0, self.up).wait_recv()
        self.copy(self.half(self.left, 0), 2, self.up).start()

    def forward_right(self):
        self.copy(self.piece(self.right), 1, self.down).wait_recv()
        self.copy(self.half(self.right, 1), 3, self.down).start()

    def finish(self):
        self.copy(self.half(self.opp, 0), 2, self.up).wait_recv()
        self.copy(self.half(self.opp, 1), 3, self.down).wait_recv()

    def drain(self):
        self.copy(self.piece(self.at), 0, self.up).wait_send()
        self.copy(self.piece(self.at), 1, self.down).wait_send()
        self.copy(self.half(self.left, 0), 2, self.up).wait_send()
        self.copy(self.half(self.right, 1), 3, self.down).wait_send()


class Spread:
    def __init__(self, piece, at, devs, send, recv):
        self.piece, self.devs, self.send, self.recv = piece, devs, send, recv
        self.places = [lax.rem(at + d, 4) for d in (0, 3, 1, 2)]

    def copy(self, place, n):
        ref = self.piece(place)
        return pltpu.make_async_remote_copy(
            src_ref=ref, dst_ref=ref, send_sem=self.send(n), recv_sem=self.recv(n),
            device_id=self.devs[n], device_id_type=MESH,
        )

    def start(self):
        for n in range(3):
            self.copy(self.places[0], n).start()

    def wait(self, n):
        self.copy(self.places[n + 1], n).wait_recv()

    def drain(self):
        for n in range(3):
            self.copy(self.places[0], n).wait_send()


def nt(a, b):
    return lax.dot_general(a, b, (((1,), (1,)), ((), ())), preferred_element_type=F32)


def nn(a, b):
    return jnp.dot(a, b, preferred_element_type=F32)


def kernel(
    table_in, lengths, store, new_hidden, wq, wk, wv, norm_gain_in, q_gain_in, k_gain_in, cosr_in, sinr_in, cosp_in, sinp_in,
    out,
    X, W, WQB, WKB, WVB, ACC, NH, SSQ, INV, OPPS, OPPR, MIDS, MIDR, KB, VB, NEWCTX, QA, QB, CTX,
    S0, R0, S1O, R1O, S1M, R1M, A1, R2M, FIN, TV, TS,
    table, norm_gain, q_gain, k_gain, cosr, sinr, cosp, sinp,
    lsem, wbsem, w1s, w1r, w2s, w2r, w3s, w3r, nhs, nhr, sqs, sqr, os_, or_, ms, mr,
    q1s, q1r, q2s, q2r, q3s, q3r, c0s, c0r, c1os, c1or, c1ms, c1mr, c2s, c2r,
):
    QS = (QA, QB)
    p = lax.axis_index("pool")
    z = lax.axis_index("tensor")
    c = lax.rem(p, 2)
    x = lax.rem(p // 2, 4)
    y = p // 8
    oc = 1 - c

    def at(yy, xx, cc):
        return yy * 8 + xx * 2 + cc

    def rot(v, d):
        return lax.rem(v + d, 4)

    zdev = [(p, rot(z, d)) for d in range(4)]
    xup, xdn = (at(y, rot(x, 1), c), z), (at(y, rot(x, 3), c), z)
    yup, ydn = (at(rot(y, 1), x, c), z), (at(rot(y, 3), x, c), z)
    sib = (at(y, x, oc), z)
    xall = (xup, xdn, (at(y, rot(x, 2), c), z))
    yall = (yup, ydn, (at(rot(y, 2), x, c), z))

    def rcopy(src, dst, ss, rs, dev):
        return pltpu.make_async_remote_copy(
            src_ref=src, dst_ref=dst, send_sem=ss, recv_sem=rs, device_id=dev, device_id_type=MESH
        )

    ld_new = pltpu.make_async_copy(new_hidden, NH.at[z], lsem.at[0])
    ld_new.start()
    ld_x = [pltpu.make_async_copy(store.at[pl.ds(6 * n, 6)], X.at[pl.ds(6 * n, 6)], lsem.at[1 + n]) for n in range(2)]
    for cp in ld_x:
        cp.start()

    small = [
        (table_in, table), (norm_gain_in, norm_gain), (q_gain_in, q_gain), (k_gain_in, k_gain),
        (cosr_in, cosr), (sinr_in, sinr), (cosp_in, cosp), (sinp_in, sinp),
    ]
    ld_small = [pltpu.make_async_copy(src, dst, lsem.at[8 + n]) for n, (src, dst) in enumerate(small)]
    for cp in ld_small:
        cp.start()

    barrier = pltpu.get_barrier_semaphore()
    peers = [*zdev[1:], *xall, *yall, sib]
    for dev in peers:
        pl.semaphore_signal(barrier, inc=1, device_id=dev, device_id_type=MESH)

    def block_loads(d):
        rows = pl.ds(pl.multiple_of(rot(z, d) * FEAT, FEAT), FEAT)
        b = (0, 1, 1, 0)[d]
        return [
            pltpu.make_async_copy(wq.at[rows, :], WQB.at[b], wbsem.at[b, 0]),
            pltpu.make_async_copy(wk.at[rows, :], WKB.at[b], wbsem.at[b, 1]),
            pltpu.make_async_copy(wv.at[rows, :], WVB.at[b], wbsem.at[b, 2]),
        ]

    own_rows = pl.ds(pl.multiple_of(z * FEAT, FEAT), FEAT)
    ld_w = []
    for h in range(2):
        for kv, ref in enumerate((wk, wv)):
            ld_w.append(
                pltpu.make_async_copy(
                    ref.at[own_rows, h * HD : (h + 1) * HD], W.at[0, h, kv], lsem.at[4 + 2 * h + kv]
                )
            )

    pl.semaphore_wait(barrier, len(peers))
    ring_at = (x, y)

    def seg_rows(cc, k):
        return pl.ds(pl.multiple_of(cc * (4 * SEG) + k * SEG, SEG), SEG)

    def w1_copy(e, h, kv):
        ref = (wk, wv)[kv]
        seg = pl.multiple_of(c * (4 * SEG) + ring_at[kv] * SEG, SEG)
        src = ref.at[pl.ds(pl.multiple_of(rot(z, e) * FEAT + seg, SEG), SEG), h * HD : (h + 1) * HD]
        return rcopy(src, W.at[4 - e, h, kv, pl.ds(seg, SEG), :], w1s.at[kv, h, e], w1r.at[kv, h, 4 - e], zdev[e])

    nh_ring = Ring(
        lambda k: NH.at[k], lambda k, s: NH.at[k, pl.ds(64 * s, 64), :], z, zdev[1], zdev[3],
        lambda k: nhs.at[k], lambda k: nhr.at[k],
    )
    def w1_start(h):
        for kv in range(2):
            for e in (2, 1, 3):
                w1_copy(e, h, kv).start()

    w1_start(0)

    def w1_wait(slot, h, kv):
        seg = pl.multiple_of(c * (4 * SEG) + ring_at[kv] * SEG, SEG)
        dst = W.at[slot, h, kv, pl.ds(seg, SEG), :]
        rcopy(dst, dst, w1s.at[kv, h, slot], w1r.at[kv, h, slot], zdev[slot]).wait_recv()

    for cp in ld_small:
        cp.wait()
    page = table[...] - p * PAGES
    hit = jnp.logical_and(page >= 0, page < PAGES)
    rank = lax.broadcasted_iota(jnp.int32, (16, REQS), 0)
    slots = PAGES + jnp.sum(jnp.where(hit, page - PAGES, 0), axis=0, keepdims=True)
    askers = jnp.where(slots == rank, lax.broadcasted_iota(jnp.int32, (16, REQS), 1), 0)
    TV[...] = jnp.zeros_like(TV)
    TV[0:1, :REQS] = jnp.clip(slots, 0, PAGES)
    TV[1:2, :REQS] = jnp.clip(jnp.sum(jnp.where(hit, rank, 0), axis=0, keepdims=True), 0, 15)
    TV[8:24, :] = jnp.broadcast_to(jnp.clip(jnp.sum(askers, axis=1, keepdims=True), 0, REQS - 1), (16, HD))
    to_scalar = pltpu.make_async_copy(TV, TS, lsem.at[3])
    to_scalar.start()

    CTX[0, PAGES] = jnp.zeros((2, HALF, HD), BF16)
    CTX[1, PAGES] = jnp.zeros((2, HALF, HD), BF16)

    lane = lax.broadcasted_iota(jnp.int32, (ROWS, ROWS), 1)
    row = lax.broadcasted_iota(jnp.int32, (ROWS, ROWS), 0)
    eye = lane == row

    def gain_of(zz):
        return jnp.concatenate([norm_gain[pl.ds(zz * (FEAT // HD) + k, 1), :] for k in range(FEAT // HD)], axis=1)


    def squares_of(v):
        v = v.astype(F32)
        return jnp.sum(v * v, axis=1, keepdims=True)

    ld_new.wait()
    squares = jnp.where(lane == PAGES, squares_of(NH[z]), 0.0)
    for n in range(2):
        ld_x[n].wait()
        squares = lax.fori_loop(
            6 * n, 6 * n + 6, lambda j, acc: jnp.where(lane == j, squares_of(X[j]), acc), squares
        )
    SSQ[z] = jnp.transpose(squares)[:16, :]
    for e in (1, 2, 3):
        rcopy(SSQ.at[z], SSQ.at[z], sqs.at[e], sqr.at[e], zdev[e]).start()
    nh_ring.start()
    w1_start(1)
    to_scalar.wait()

    for d in (0, 1):
        for cp in block_loads(d):
            cp.start()
    for cp in ld_w:
        cp.start()

    def normed(v, j, gain):
        inv = jnp.sum(jnp.where(lane == j, INV[...], 0.0), axis=1, keepdims=True)
        return (v.astype(F32) * inv * gain).astype(BF16)

    def prepare(j, carry):
        X[j] = normed(X[j], j, gain)
        return carry

    def w_piece(h, kv, cc):
        return lambda k: W.at[pl.ds(1, 3), h, kv, seg_rows(cc, k), :]

    def w_spread_of(h, kv):
        return Spread(
            w_piece(h, kv, c), ring_at[kv], (xall, yall)[kv], lambda n: w2s.at[h, kv, n], lambda n: w2r.at[h, kv, n]
        )

    w_spread = [[w_spread_of(h, kv) for kv in range(2)] for h in range(2)]

    def w3_copy(h, kv, cc, n):
        ref = w_piece(h, kv, cc)(w_spread[h][kv].places[n])
        return rcopy(ref, ref, w3s.at[h, kv, n], w3r.at[h, kv, n], sib)

    def w_start(h):
        for kv in range(2):
            for slot in (1, 2, 3):
                w1_wait(slot, h, kv)
            w_spread[h][kv].start()
            w3_copy(h, kv, c, 0).start()

    def w_share(h):
        for n in range(3):
            for kv in range(2):
                w_spread[h][kv].wait(n)
                w3_copy(h, kv, c, n + 1).start()

    def w_wait(h):
        for kv in range(2):
            for n in range(4):
                w3_copy(h, kv, oc, n).wait_recv()
            ld_w[2 * h + kv].wait()

    sign = jnp.where(lax.broadcasted_iota(jnp.int32, (1, HD), 1) < HD // 2, -1.0, 1.0).astype(F32)
    cos_r, sin_r = cosr[...], sinr[...]

    def angle_at(first_cos, first_sin):
        return first_cos * cos_r - first_sin * sin_r, (first_sin * cos_r + first_cos * sin_r) * sign

    def normed_rope(v, g, cos, sin):
        v = v * lax.rsqrt(jnp.mean(v * v, axis=1, keepdims=True) + EPS) * g
        return (v * cos + pltpu.roll(v, HD // 2, 1) * sin).astype(BF16)

    def project_new(d):
        for cp in block_loads(d):
            cp.wait()
        b = (0, 1, 1, 0)[d]
        a = normed(NH[rot(z, d)], PAGES, gain_of(rot(z, d)))
        parts = ((0, WQB), (1024, WKB), (1280, WVB))
        for first, ref in parts:
            width = ref.shape[2]
            prod = nn(a, ref[b])
            if d == 0:
                ACC[:, first : first + width] = prod
            else:
                ACC[:, first : first + width] += prod
        if d < 2:
            for cp in block_loads(3 - d):
                cp.start()

    w_start(0)
    for e in (1, 2, 3):
        far = SSQ.at[rot(z, 4 - e)]
        rcopy(far, far, sqs.at[e], sqr.at[e], zdev[e]).wait_recv()
    total = SSQ[0] + SSQ[1] + SSQ[2] + SSQ[3]
    inverse = lax.rsqrt(total * (1.0 / WIDE) + EPS)
    INV[...] = jnp.transpose(jnp.concatenate([inverse, jnp.zeros((ROWS - 16, ROWS), F32)], axis=0))

    gain = gain_of(z)
    lax.fori_loop(0, PAGES, prepare, 0)
    project_new(0)
    nh_ring.forward_left()
    nh_ring.forward_right()
    w_share(0)
    w_wait(0)

    def product(i, slot):
        h, pair = i // 6, lax.rem(i, 6)
        a = X[pl.ds(pair * 2, 2)].reshape(2 * ROWS, FEAT)
        return nn(a, jnp.concatenate([W[slot, h, 0], W[slot, h, 1]], axis=1))

    def opp_copy(i, s):
        return rcopy(OPPS.at[i, s], OPPR.at[i, s], os_.at[i, s], or_.at[i, s], (zdev[1], zdev[3])[s])

    def mid_copy(i, s):
        return rcopy(MIDS.at[i, s], MIDR.at[i, s], ms.at[i, s], mr.at[i, s], (zdev[1], zdev[3])[s])

    def opposite(i):
        part = product(i, 2).astype(BF16)
        for s in range(2):
            OPPS[i, s] = part[s * ROWS : (s + 1) * ROWS]
            opp_copy(i, s).start()

    def neighbours(i):
        for s in range(2):
            part = product(i, (1, 3)[s])
            opp_copy(i, s).wait_recv()
            for t in range(2):
                page = part[t * ROWS : (t + 1) * ROWS]
                if t == s:
                    page = page + OPPR[i, s].astype(F32)
                MIDS[i, s, t] = page.astype(BF16)
            mid_copy(i, s).start()

    def own(i):
        h, pair = i // 6, lax.rem(i, 6)
        part = product(i, 0)
        for s in range(2):
            mid_copy(i, s).wait_recv()
        for t in range(2):
            j = pair * 2 + t
            page = part[t * ROWS : (t + 1) * ROWS] + MIDR[i, 0, t].astype(F32) + MIDR[i, 1, t].astype(F32)
            n = h * PAGES + j
            request = TS[8 + j, 0]
            i_page = TS[1, request]
            cos, sin = angle_at(cosp[pl.ds(i_page, 1), :], sinp[pl.ds(i_page, 1), :])
            KB[n] = normed_rope(page[:, :HD], k_gain[...], cos, sin)
            live = row < lengths[request] - i_page * ROWS
            VB[n, :, :HD] = jnp.where(live, page[:, HD:], 0.0).astype(BF16)
            VB[n, :, HD:] = jnp.where(live, 1.0, 0.0).astype(BF16)

    def attend(h, j):
        n = h * PAGES + j
        request = TS[8 + j, 0]
        core, xx, yy = lax.rem(request, 2), lax.rem(request // 2, 4), request // 8
        query = jnp.concatenate(
            [QS[h][0, core * 16 + yy * 4 + xx], QS[h][1, core * 16 + xx * 4 + yy]], axis=0
        )
        scores = nt(query, KB[n]) * SCALE
        mixed = nn(jnp.exp(scores).astype(BF16), VB[n])
        line = lax.broadcasted_iota(jnp.int32, (16, HD), 0)
        for s in range(2):
            CTX[h, j, s, :256, :] = mixed[s * 256 : (s + 1) * 256, :HD].astype(BF16)
            sums = []
            for g in range(2):
                block = mixed[s * 256 + g * ROWS : s * 256 + (g + 1) * ROWS, HD:]
                sums.append(jnp.sum(jnp.where(eye, block, 0.0), axis=0, keepdims=True))
            CTX[h, j, s, 256:, :] = jnp.where(line == 0, sums[0], jnp.where(line == 1, sums[1], 0.0)).astype(BF16)

    def attend_pages(h, first, last):
        def one(j, carry):
            attend(h, j)
            return carry

        lax.fori_loop(first, last, one, 0)

    q_at = (c * 16 + y * 4 + x, c * 16 + x * 4 + y)

    def q1_of(h, s):
        base = c * 16 + (y * 4, x * 4)[s]
        return Spread(
            lambda k: QS[h].at[s, base + k], (x, y)[s], (xall, yall)[s], lambda n: q1s.at[h, s, n], lambda n: q1r.at[h, s, n]
        )

    def q2_of(h, s):
        return Spread(
            lambda k: QS[h].at[s, pl.ds(c * 16 + k * 4, 4)], (y, x)[s], (yall, xall)[s],
            lambda n: q2s.at[h, s, n], lambda n: q2r.at[h, s, n],
        )

    q1 = [[q1_of(h, s) for s in range(2)] for h in range(2)]
    q2 = [[q2_of(h, s) for s in range(2)] for h in range(2)]

    def q3_copy(h, s, cc, n):
        ref = QS[h].at[s, pl.ds(cc * 16 + q2[h][s].places[n] * 4, 4)]
        return rcopy(ref, ref, q3s.at[h, s, n], q3r.at[h, s, n], sib)

    def angles_new():
        length = lengths[p]
        page_cos, page_sin = cosp[pl.ds(length // ROWS, 1), :], sinp[pl.ds(length // ROWS, 1), :]
        rest_cos, rest_sin = cosr[pl.ds(lax.rem(length, ROWS), 1), :], sinr[pl.ds(lax.rem(length, ROWS), 1), :]
        return angle_at(page_cos * rest_cos - page_sin * rest_sin, page_sin * rest_cos + page_cos * rest_sin)

    def q_begin():
        nh_ring.finish()
        project_new(2)
        cos_new, sin_new = angles_new()
        for h in range(2):
            for s in range(2):
                for g in range(2):
                    n = h * GROUP + s * 2 + g
                    raw = ACC[:, n * HD : (n + 1) * HD]
                    QS[h][s, q_at[s], g * ROWS : (g + 1) * ROWS, :] = normed_rope(raw, q_gain[...], cos_new, sin_new)
                q1[h][s].start()

    def q_along(h):
        for s in range(2):
            for n in range(3):
                q1[h][s].wait(n)
            q2[h][s].start()
            q3_copy(h, s, c, 0).start()

    def q_share(h):
        for n in range(3):
            for s in range(2):
                q2[h][s].wait(n)
                q3_copy(h, s, c, n + 1).start()

    def q_wait(h):
        for s in range(2):
            for n in range(4):
                q3_copy(h, s, oc, n).wait_recv()

    def attend_new():
        cos_new, sin_new = angles_new()
        causal = lax.broadcasted_iota(jnp.int32, (QROWS, ROWS), 1) <= (
            lax.broadcasted_iota(jnp.int32, (QROWS, ROWS), 0) & (ROWS - 1)
        )
        ones = jnp.ones((ROWS, HD), BF16)
        for h in range(2):
            key = normed_rope(ACC[:, 1024 + h * HD : 1024 + (h + 1) * HD], k_gain[...], cos_new, sin_new)
            val = ACC[:, 1280 + h * HD : 1280 + (h + 1) * HD].astype(BF16)
            query = jnp.concatenate([QS[h][0, q_at[0]], QS[h][1, q_at[1]]], axis=0)
            scores = nt(query, key) * SCALE
            weights = jnp.where(causal, jnp.exp(scores), 0.0).astype(BF16)
            NEWCTX[h] = nn(weights, jnp.concatenate([val, ones], axis=1))

    first_dev = ((xup, xdn), (yup, ydn))
    last_dev = (yall, xall)
    first_at, last_at = (x, y), (y, x)

    def mine(h, s, o, b, core):
        a = rot(first_at[s], o)
        chip = b * 4 + a if s == 0 else a * 4 + b
        return CTX[h, TS[0, chip * 2 + core], s]

    def value(h, s, o, b):
        return mine(h, s, o, b, c) + R0[h, s, o, b]

    def c0_copy(h, s, o):
        return rcopy(S0.at[s, o], R0.at[h, s, o], c0s.at[h, s, o], c0r.at[h, s, o], sib)

    def c0(h):
        for o in (2, 1, 3, 0):
            for s in range(2):

                def fill(b, carry):
                    S0[s, o, b] = mine(h, s, o, b, oc)
                    return carry

                lax.fori_loop(0, 4, fill, 0)
                c0_copy(h, s, o).start()

    def c1o_copy(h, s, d):
        part = pl.ds(d * 2, 2)
        return rcopy(S1O.at[h, s, part], R1O.at[h, s, part], c1os.at[h, s, d], c1or.at[h, s, d], first_dev[s][d])

    def c1m_copy(h, s, d, n):
        part = pl.ds(n * 2, 2)
        return rcopy(
            S1M.at[h, s, d, part], R1M.at[h, s, d, part], c1ms.at[h, s, d, n], c1mr.at[h, s, d, n], first_dev[s][d]
        )

    def c2_copy(h, s, n):
        src = A1.at[h, s, (1, 3, 2)[n]]
        return rcopy(src, R2M.at[h, s, n], c2s.at[h, s, n], c2r.at[h, s, n], last_dev[s][n])

    def c1(h):
        for s in range(2):
            c0_copy(h, s, 2).wait_recv()

            def fill(b, carry):
                S1O[h, s, b] = value(h, s, 2, b)
                return carry

            lax.fori_loop(0, 4, fill, 0)
            for d in range(2):
                c1o_copy(h, s, d).start()
        for d in range(2):
            for s in range(2):
                o, n = (1, 3)[d], 1 - d
                c0_copy(h, s, o).wait_recv()

                def fill(b, carry):
                    S1M[h, s, d, b] = value(h, s, o, b)
                    return carry

                lax.fori_loop(n * 2, n * 2 + 2, fill, 0)
                c1m_copy(h, s, d, n).start()

    def c2(h):
        for d in range(2):
            for s in range(2):
                o = (1, 3)[d]
                c1o_copy(h, s, d).wait_recv()

                def fill(b, carry):
                    S1M[h, s, d, b] = value(h, s, o, b) + R1O[h, s, b]
                    return carry

                lax.fori_loop(d * 2, d * 2 + 2, fill, 0)
                c1m_copy(h, s, d, d).start()

    def c3(h):
        for s in range(2):
            c0_copy(h, s, 0).wait_recv()
            for d in range(2):
                for n in range(2):
                    c1m_copy(h, s, d, n).wait_recv()

            for n, o in ((2, 2), (0, 1), (1, 3), (None, 0)):
                b = rot(last_at[s], o)
                A1[h, s, o] = value(h, s, 0, b) + R1M[h, s, 0, b] + R1M[h, s, 1, b]
                if n is not None:
                    c2_copy(h, s, n).start()

    def c4(h):
        for s in range(2):
            for n in range(3):
                c2_copy(h, s, n).wait_recv()
            parts = R2M[h, s, 0].astype(F32) + R2M[h, s, 1].astype(F32) + R2M[h, s, 2].astype(F32)
            FIN[...] = A1[h, s, 0].astype(F32) + parts
            for g in range(2):
                n = s * 2 + g
                mixed = FIN[g * ROWS : (g + 1) * ROWS, :] + NEWCTX[h, n * ROWS : (n + 1) * ROWS, :HD]
                sums = jnp.sum(jnp.where(eye, FIN[256 + g : 257 + g, :], 0.0), axis=1, keepdims=True)
                sums = sums + NEWCTX[h, n * ROWS : (n + 1) * ROWS, HD:]
                m = h * GROUP + n
                out[:, m * HD : (m + 1) * HD] = (mixed / sums).astype(BF16)

    opposite(0)
    opposite(1)
    w_start(1)
    project_new(1)
    project_new(3)

    def step(i, carry):
        def at_step(k, *actions):
            @pl.when(i == k)
            def _():
                for action in actions:
                    action()

        @pl.when(i < ITEMS - 2)
        def _():
            opposite(i + 2)

        @pl.when(i < ITEMS)
        def _():
            neighbours(i)

        @pl.when(i >= 2)
        def _():
            own(i - 2)

        def pages(h, first, last):
            return lambda: attend_pages(h, first, last)

        def of(stage, h):
            return lambda: stage(h)

        at_step(0, q_begin)
        at_step(1, of(w_share, 1))
        at_step(2, of(q_along, 0))
        at_step(3, of(w_wait, 1), attend_new)
        at_step(4, of(q_along, 1))
        at_step(5, of(q_share, 0))
        at_step(6, of(q_wait, 0), pages(0, 0, 6))
        at_step(7, pages(0, 6, 12), of(c0, 0))
        at_step(8, of(c1, 0), of(q_share, 1))
        at_step(9, of(q_wait, 1), pages(1, 0, 3))
        at_step(10, of(c2, 0), pages(1, 3, 6))
        at_step(11, pages(1, 6, 8))
        at_step(12, of(c3, 0), pages(1, 8, 10))
        at_step(13, pages(1, 10, 12))
        return carry

    lax.fori_loop(0, ITEMS + 2, step, 0)
    for o in range(4):
        for s in range(2):
            c0_copy(0, s, o).wait_send()
    c0(1)
    c1(1)
    c4(0)
    c2(1)
    c3(1)
    c4(1)

    for kv in range(2):
        for h in range(2):
            for e in (1, 2, 3):
                w1_copy(e, h, kv).wait_send()
            w_spread[h][kv].drain()
            for n in range(4):
                w3_copy(h, kv, c, n).wait_send()
    nh_ring.drain()
    for e in (1, 2, 3):
        rcopy(SSQ.at[z], SSQ.at[z], sqs.at[e], sqr.at[e], zdev[e]).wait_send()

    def drain(i, carry):
        for s in range(2):
            opp_copy(i, s).wait_send()
            mid_copy(i, s).wait_send()
        return carry

    lax.fori_loop(0, ITEMS, drain, 0)
    for o in range(4):
        for s in range(2):
            c0_copy(1, s, o).wait_send()
    for h in range(2):
        for s in range(2):
            q1[h][s].drain()
            q2[h][s].drain()
            for n in range(4):
                q3_copy(h, s, c, n).wait_send()
            for d in range(2):
                c1o_copy(h, s, d).wait_send()
                for n in range(2):
                    c1m_copy(h, s, d, n).wait_send()
            for n in range(3):
                c2_copy(h, s, n).wait_send()


def local(store, new_hidden, wq, wk, wv, norm_gain, q_gain, k_gain, page_table, hist_len):
    tables = [jnp.asarray(t) for t in rope_tables()]
    vm = pl.BlockSpec(memory_space=pltpu.VMEM)
    hbm = pl.BlockSpec(memory_space=pl.ANY)
    dma = pltpu.SemaphoreType.DMA
    scratch = [
        pltpu.VMEM((PAGES, ROWS, FEAT), BF16),
        pltpu.VMEM((4, 2, 2, FEAT, HD), BF16),
        pltpu.VMEM((2, FEAT, 1024), BF16),
        pltpu.VMEM((2, FEAT, 256), BF16),
        pltpu.VMEM((2, FEAT, 256), BF16),
        pltpu.VMEM((ROWS, 1536), F32),
        pltpu.VMEM((4, ROWS, FEAT), BF16),
        pltpu.VMEM((4, 16, ROWS), F32),
        pltpu.VMEM((ROWS, ROWS), F32),
        pltpu.VMEM((ITEMS, 2, ROWS, 256), BF16),
        pltpu.VMEM((ITEMS, 2, ROWS, 256), BF16),
        pltpu.VMEM((ITEMS, 2, 2, ROWS, 256), BF16),
        pltpu.VMEM((ITEMS, 2, 2, ROWS, 256), BF16),
        pltpu.VMEM((2 * PAGES, ROWS, HD), BF16),
        pltpu.VMEM((2 * PAGES, ROWS, 2 * HD), BF16),
        pltpu.VMEM((2, QROWS, 2 * HD), F32),
        pltpu.VMEM((2, REQS, QROWS // 2, HD), BF16),
        pltpu.VMEM((2, REQS, QROWS // 2, HD), BF16),
        pltpu.VMEM((2, PAGES + 1, 2, HALF, HD), BF16),
        pltpu.VMEM((2, 4, 4, HALF, HD), BF16),
        pltpu.VMEM((2, 2, 4, 4, HALF, HD), BF16),
        pltpu.VMEM((2, 2, 4, HALF, HD), BF16),
        pltpu.VMEM((2, 2, 4, HALF, HD), BF16),
        pltpu.VMEM((2, 2, 2, 4, HALF, HD), BF16),
        pltpu.VMEM((2, 2, 2, 4, HALF, HD), BF16),
        pltpu.VMEM((2, 2, 4, HALF, HD), BF16),
        pltpu.VMEM((2, 2, 3, HALF, HD), BF16),
        pltpu.VMEM((HALF, HD), F32),
        pltpu.VMEM((24, HD), jnp.int32),
        pltpu.SMEM((24, HD), jnp.int32),
        pltpu.VMEM((16, REQS), jnp.int32),
        pltpu.VMEM((WIDE // HD, HD), F32),
        pltpu.VMEM((1, HD), F32),
        pltpu.VMEM((1, HD), F32),
        pltpu.VMEM((ROWS, HD), F32),
        pltpu.VMEM((ROWS, HD), F32),
        pltpu.VMEM((24, HD), F32),
        pltpu.VMEM((24, HD), F32),
        dma((16,)), dma((2, 3)),
        dma((2, 2, 4)), dma((2, 2, 4)), dma((2, 2, 4)), dma((2, 2, 4)), dma((2, 2, 4)), dma((2, 2, 4)),
        dma((4,)), dma((4,)), dma((4,)), dma((4,)),
        dma((ITEMS, 2)), dma((ITEMS, 2)), dma((ITEMS, 2)), dma((ITEMS, 2)),
        dma((2, 2, 4)), dma((2, 2, 4)), dma((2, 2, 4)), dma((2, 2, 4)), dma((2, 2, 4)), dma((2, 2, 4)),
        dma((2, 2, 4)), dma((2, 2, 4)),
        dma((2, 2, 2)), dma((2, 2, 2)), dma((2, 2, 2, 2)), dma((2, 2, 2, 2)),
        dma((2, 2, 3)), dma((2, 2, 3)),
    ]
    return pl.pallas_call(
        kernel,
        out_shape=jax.ShapeDtypeStruct((ROWS, 2 * GROUP * HD), BF16),
        in_specs=[hbm, pl.BlockSpec(memory_space=pltpu.SMEM)] + [hbm] * 12,
        out_specs=vm,
        scratch_shapes=scratch,
        compiler_params=pltpu.CompilerParams(
            collective_id=0, has_side_effects=True, vmem_limit_bytes=63 * 1024 * 1024
        ),
        cost_estimate=pl.CostEstimate(flops=12_000_000_000, bytes_accessed=25_000_000, transcendentals=2_000_000),
    )(
        page_table.T, hist_len, store, new_hidden, wq, wk, wv, norm_gain.reshape(WIDE // HD, HD),
        q_gain.reshape(1, HD), k_gain.reshape(1, HD), *tables,
    )


def solution(mesh):
    return jax.shard_map(
        local,
        mesh=mesh,
        in_specs=(
            P("pool", None, "tensor"),
            P("pool", "tensor"),
            P(None, "tensor"),
            P(None, "tensor"),
            P(None, "tensor"),
            P(),
            P(),
            P(),
            P(),
            P(),
        ),
        out_specs=P("pool", "tensor"),
        check_vma=False,
    )
```

```python
import jax
import jax.numpy as jnp
import numpy as np
from jax import lax
from jax.experimental import pallas as pl
from jax.experimental.pallas import tpu as pltpu
from jax.sharding import PartitionSpec as P

EPS = 1e-06
ROPE_BASE = 1000000.0
MESH = pl.DeviceIdType.MESH
F32 = jnp.float32
BF16 = jnp.bfloat16

PAGES = 12
ROWS = 128
FEAT = 1280
NZ = 4
WIDE = FEAT * NZ
HD = 128
GROUP = 4
QROWS = GROUP * ROWS
REQS = 32
ITEMS = 12
HALF = 272
SEG = 160
SCALE = HD ** -0.5


def rope_tables():
    freq = ROPE_BASE ** (-np.arange(64, dtype=np.float64) * 2.0 / HD)
    freq = np.concatenate([freq, freq])[None, :]
    rows = np.arange(ROWS, dtype=np.float64)[:, None] * freq
    pages = np.arange(24, dtype=np.float64)[:, None] * ROWS * freq
    return [np.asarray(t, np.float32) for t in (np.cos(rows), np.sin(rows), np.cos(pages), np.sin(pages))]


class Ring:
    def __init__(self, piece, half, at, dev_up, dev_down, send, recv):
        self.piece, self.half, self.at = piece, half, at
        self.up, self.down, self.send, self.recv = dev_up, dev_down, send, recv
        self.left = lax.rem(at + 3, 4)
        self.right = lax.rem(at + 1, 4)
        self.opp = lax.rem(at + 2, 4)

    def copy(self, ref, k, dev):
        return pltpu.make_async_remote_copy(
            src_ref=ref, dst_ref=ref, send_sem=self.send(k), recv_sem=self.recv(k), device_id=dev, device_id_type=MESH
        )

    def start(self):
        self.copy(self.piece(self.at), 0, self.up).start()
        self.copy(self.piece(self.at), 1, self.down).start()

    def forward_left(self):
        self.copy(self.piece(self.left), 0, self.up).wait_recv()
        self.copy(self.half(self.left, 0), 2, self.up).start()

    def forward_right(self):
        self.copy(self.piece(self.right), 1, self.down).wait_recv()
        self.copy(self.half(self.right, 1), 3, self.down).start()

    def finish(self):
        self.copy(self.half(self.opp, 0), 2, self.up).wait_recv()
        self.copy(self.half(self.opp, 1), 3, self.down).wait_recv()

    def drain(self):
        self.copy(self.piece(self.at), 0, self.up).wait_send()
        self.copy(self.piece(self.at), 1, self.down).wait_send()
        self.copy(self.half(self.left, 0), 2, self.up).wait_send()
        self.copy(self.half(self.right, 1), 3, self.down).wait_send()


class Spread:
    def __init__(self, piece, at, devs, send, recv):
        self.piece, self.devs, self.send, self.recv = piece, devs, send, recv
        self.places = [lax.rem(at + d, 4) for d in (0, 3, 1, 2)]

    def copy(self, place, n):
        ref = self.piece(place)
        return pltpu.make_async_remote_copy(
            src_ref=ref, dst_ref=ref, send_sem=self.send(n), recv_sem=self.recv(n),
            device_id=self.devs[n], device_id_type=MESH,
        )

    def start(self):
        for n in range(3):
            self.copy(self.places[0], n).start()

    def wait(self, n):
        self.copy(self.places[n + 1], n).wait_recv()

    def drain(self):
        for n in range(3):
            self.copy(self.places[0], n).wait_send()


def nt(a, b):
    return lax.dot_general(a, b, (((1,), (1,)), ((), ())), preferred_element_type=F32)


def nn(a, b):
    return jnp.dot(a, b, preferred_element_type=F32)


def kernel(
    table_in, lengths, store, new_hidden, wq, wk, wv, norm_gain_in, q_gain_in, k_gain_in, cosr_in, sinr_in, cosp_in, sinp_in,
    out,
    X, W, WQB, WKB, WVB, ACC, NH, SSQ, INV, OPPS, OPPR, MIDS, MIDR, KB, VB, NEWCTX, QA, QB, CTX,
    S0, R0, S1O, R1O, S1M, R1M, A1, R2M, FIN, TV, TS,
    table, norm_gain, q_gain, k_gain, cosr, sinr, cosp, sinp,
    lsem, wbsem, w1s, w1r, w2s, w2r, w3s, w3r, nhs, nhr, sqs, sqr, os_, or_, ms, mr,
    q1s, q1r, q2s, q2r, q3s, q3r, c0s, c0r, c1os, c1or, c1ms, c1mr, c2s, c2r,
):
    QS = (QA, QB)
    p = lax.axis_index("pool")
    z = lax.axis_index("tensor")
    c = lax.rem(p, 2)
    x = lax.rem(p // 2, 4)
    y = p // 8
    oc = 1 - c

    def at(yy, xx, cc):
        return yy * 8 + xx * 2 + cc

    def rot(v, d):
        return lax.rem(v + d, 4)

    zdev = [(p, rot(z, d)) for d in range(4)]
    xup, xdn = (at(y, rot(x, 1), c), z), (at(y, rot(x, 3), c), z)
    yup, ydn = (at(rot(y, 1), x, c), z), (at(rot(y, 3), x, c), z)
    sib = (at(y, x, oc), z)
    xall = (xup, xdn, (at(y, rot(x, 2), c), z))
    yall = (yup, ydn, (at(rot(y, 2), x, c), z))

    def rcopy(src, dst, ss, rs, dev):
        return pltpu.make_async_remote_copy(
            src_ref=src, dst_ref=dst, send_sem=ss, recv_sem=rs, device_id=dev, device_id_type=MESH
        )

    ld_new = pltpu.make_async_copy(new_hidden, NH.at[z], lsem.at[0])
    ld_new.start()
    ld_x = [pltpu.make_async_copy(store.at[pl.ds(6 * n, 6)], X.at[pl.ds(6 * n, 6)], lsem.at[1 + n]) for n in range(2)]
    for cp in ld_x:
        cp.start()

    small = [
        (table_in, table), (norm_gain_in, norm_gain), (q_gain_in, q_gain), (k_gain_in, k_gain),
        (cosr_in, cosr), (sinr_in, sinr), (cosp_in, cosp), (sinp_in, sinp),
    ]
    ld_small = [pltpu.make_async_copy(src, dst, lsem.at[8 + n]) for n, (src, dst) in enumerate(small)]
    for cp in ld_small:
        cp.start()

    barrier = pltpu.get_barrier_semaphore()
    peers = [*zdev[1:], *xall, *yall, sib]
    for dev in peers:
        pl.semaphore_signal(barrier, inc=1, device_id=dev, device_id_type=MESH)

    def block_loads(d):
        rows = pl.ds(pl.multiple_of(rot(z, d) * FEAT, FEAT), FEAT)
        b = (0, 1, 1, 0)[d]
        return [
            pltpu.make_async_copy(wq.at[rows, :], WQB.at[b], wbsem.at[b, 0]),
            pltpu.make_async_copy(wk.at[rows, :], WKB.at[b], wbsem.at[b, 1]),
            pltpu.make_async_copy(wv.at[rows, :], WVB.at[b], wbsem.at[b, 2]),
        ]

    own_rows = pl.ds(pl.multiple_of(z * FEAT, FEAT), FEAT)
    ld_w = []
    for h in range(2):
        for kv, ref in enumerate((wk, wv)):
            ld_w.append(
                pltpu.make_async_copy(
                    ref.at[own_rows, h * HD : (h + 1) * HD], W.at[0, h, kv], lsem.at[4 + 2 * h + kv]
                )
            )

    pl.semaphore_wait(barrier, len(peers))
    ring_at = (x, y)

    def seg_rows(cc, k):
        return pl.ds(pl.multiple_of(cc * (4 * SEG) + k * SEG, SEG), SEG)

    def w1_copy(e, h, kv):
        ref = (wk, wv)[kv]
        seg = pl.multiple_of(c * (4 * SEG) + ring_at[kv] * SEG, SEG)
        src = ref.at[pl.ds(pl.multiple_of(rot(z, e) * FEAT + seg, SEG), SEG), h * HD : (h + 1) * HD]
        return rcopy(src, W.at[4 - e, h, kv, pl.ds(seg, SEG), :], w1s.at[kv, h, e], w1r.at[kv, h, 4 - e], zdev[e])

    nh_ring = Ring(
        lambda k: NH.at[k], lambda k, s: NH.at[k, pl.ds(64 * s, 64), :], z, zdev[1], zdev[3],
        lambda k: nhs.at[k], lambda k: nhr.at[k],
    )
    def w1_start(h):
        for kv in range(2):
            for e in (2, 1, 3):
                w1_copy(e, h, kv).start()

    w1_start(0)

    def w1_wait(slot, h, kv):
        seg = pl.multiple_of(c * (4 * SEG) + ring_at[kv] * SEG, SEG)
        dst = W.at[slot, h, kv, pl.ds(seg, SEG), :]
        rcopy(dst, dst, w1s.at[kv, h, slot], w1r.at[kv, h, slot], zdev[slot]).wait_recv()

    for cp in ld_small:
        cp.wait()
    page = table[...] - p * PAGES
    hit = jnp.logical_and(page >= 0, page < PAGES)
    rank = lax.broadcasted_iota(jnp.int32, (16, REQS), 0)
    slots = PAGES + jnp.sum(jnp.where(hit, page - PAGES, 0), axis=0, keepdims=True)
    askers = jnp.where(slots == rank, lax.broadcasted_iota(jnp.int32, (16, REQS), 1), 0)
    TV[...] = jnp.zeros_like(TV)
    TV[0:1, :REQS] = jnp.clip(slots, 0, PAGES)
    TV[1:2, :REQS] = jnp.clip(jnp.sum(jnp.where(hit, rank, 0), axis=0, keepdims=True), 0, 15)
    TV[8:24, :] = jnp.broadcast_to(jnp.clip(jnp.sum(askers, axis=1, keepdims=True), 0, REQS - 1), (16, HD))
    to_scalar = pltpu.make_async_copy(TV, TS, lsem.at[3])
    to_scalar.start()

    CTX[0, PAGES] = jnp.zeros((2, HALF, HD), BF16)
    CTX[1, PAGES] = jnp.zeros((2, HALF, HD), BF16)

    lane = lax.broadcasted_iota(jnp.int32, (ROWS, ROWS), 1)
    row = lax.broadcasted_iota(jnp.int32, (ROWS, ROWS), 0)
    eye = lane == row

    def gain_of(zz):
        return jnp.concatenate([norm_gain[pl.ds(zz * (FEAT // HD) + k, 1), :] for k in range(FEAT // HD)], axis=1)


    def squares_of(v):
        v = v.astype(F32)
        return jnp.sum(v * v, axis=1, keepdims=True)

    ld_new.wait()
    squares = jnp.where(lane == PAGES, squares_of(NH[z]), 0.0)
    for n in range(2):
        ld_x[n].wait()
        squares = lax.fori_loop(
            6 * n, 6 * n + 6, lambda j, acc: jnp.where(lane == j, squares_of(X[j]), acc), squares
        )
    SSQ[z] = jnp.transpose(squares)[:16, :]
    for e in (1, 2, 3):
        rcopy(SSQ.at[z], SSQ.at[z], sqs.at[e], sqr.at[e], zdev[e]).start()
    nh_ring.start()
    w1_start(1)
    to_scalar.wait()

    for d in (0, 1):
        for cp in block_loads(d):
            cp.start()
    for cp in ld_w:
        cp.start()

    def normed(v, j, gain):
        inv = jnp.sum(jnp.where(lane == j, INV[...], 0.0), axis=1, keepdims=True)
        return (v.astype(F32) * inv * gain).astype(BF16)

    def prepare(j, carry):
        X[j] = normed(X[j], j, gain)
        return carry

    def w_piece(h, kv, cc):
        return lambda k: W.at[pl.ds(1, 3), h, kv, seg_rows(cc, k), :]

    def w_spread_of(h, kv):
        return Spread(
            w_piece(h, kv, c), ring_at[kv], (xall, yall)[kv], lambda n: w2s.at[h, kv, n], lambda n: w2r.at[h, kv, n]
        )

    w_spread = [[w_spread_of(h, kv) for kv in range(2)] for h in range(2)]

    def w3_copy(h, kv, cc, n):
        ref = w_piece(h, kv, cc)(w_spread[h][kv].places[n])
        return rcopy(ref, ref, w3s.at[h, kv, n], w3r.at[h, kv, n], sib)

    def w_start(h):
        for kv in range(2):
            for slot in (1, 2, 3):
                w1_wait(slot, h, kv)
            w_spread[h][kv].start()
            w3_copy(h, kv, c, 0).start()

    def w_share(h):
        for n in range(3):
            for kv in range(2):
                w_spread[h][kv].wait(n)
                w3_copy(h, kv, c, n + 1).start()

    def w_wait(h):
        for kv in range(2):
            for n in range(4):
                w3_copy(h, kv, oc, n).wait_recv()
            ld_w[2 * h + kv].wait()

    sign = jnp.where(lax.broadcasted_iota(jnp.int32, (1, HD), 1) < HD // 2, -1.0, 1.0).astype(F32)
    cos_r, sin_r = cosr[...], sinr[...]

    def angle_at(first_cos, first_sin):
        return first_cos * cos_r - first_sin * sin_r, (first_sin * cos_r + first_cos * sin_r) * sign

    def normed_rope(v, g, cos, sin):
        v = v * lax.rsqrt(jnp.mean(v * v, axis=1, keepdims=True) + EPS) * g
        return (v * cos + pltpu.roll(v, HD // 2, 1) * sin).astype(BF16)

    def project_new(d):
        for cp in block_loads(d):
            cp.wait()
        b = (0, 1, 1, 0)[d]
        a = normed(NH[rot(z, d)], PAGES, gain_of(rot(z, d)))
        parts = ((0, WQB), (1024, WKB), (1280, WVB))
        for first, ref in parts:
            width = ref.shape[2]
            prod = nn(a, ref[b])
            if d == 0:
                ACC[:, first : first + width] = prod
            else:
                ACC[:, first : first + width] += prod
        if d < 2:
            for cp in block_loads(3 - d):
                cp.start()

    w_start(0)
    for e in (1, 2, 3):
        far = SSQ.at[rot(z, 4 - e)]
        rcopy(far, far, sqs.at[e], sqr.at[e], zdev[e]).wait_recv()
    total = SSQ[0] + SSQ[1] + SSQ[2] + SSQ[3]
    inverse = lax.rsqrt(total * (1.0 / WIDE) + EPS)
    INV[...] = jnp.transpose(jnp.concatenate([inverse, jnp.zeros((ROWS - 16, ROWS), F32)], axis=0))

    gain = gain_of(z)
    lax.fori_loop(0, PAGES, prepare, 0)
    project_new(0)
    nh_ring.forward_left()
    nh_ring.forward_right()
    w_share(0)
    w_start(1)
    w_wait(0)

    def product(i, slot):
        h, pair = i // 6, lax.rem(i, 6)
        a = X[pl.ds(pair * 2, 2)].reshape(2 * ROWS, FEAT)
        return nn(a, jnp.concatenate([W[slot, h, 0], W[slot, h, 1]], axis=1))

    def opp_copy(i, s):
        return rcopy(OPPS.at[i, s], OPPR.at[i, s], os_.at[i, s], or_.at[i, s], (zdev[1], zdev[3])[s])

    def mid_copy(i, s):
        return rcopy(MIDS.at[i, s], MIDR.at[i, s], ms.at[i, s], mr.at[i, s], (zdev[1], zdev[3])[s])

    def opposite(i):
        part = product(i, 2).astype(BF16)
        for s in range(2):
            OPPS[i, s] = part[s * ROWS : (s + 1) * ROWS]
            opp_copy(i, s).start()

    def neighbours(i):
        for s in range(2):
            part = product(i, (1, 3)[s])
            opp_copy(i, s).wait_recv()
            for t in range(2):
                page = part[t * ROWS : (t + 1) * ROWS]
                if t == s:
                    page = page + OPPR[i, s].astype(F32)
                MIDS[i, s, t] = page.astype(BF16)
            mid_copy(i, s).start()

    def own(i):
        h, pair = i // 6, lax.rem(i, 6)
        part = product(i, 0)
        for s in range(2):
            mid_copy(i, s).wait_recv()
        for t in range(2):
            j = pair * 2 + t
            page = part[t * ROWS : (t + 1) * ROWS] + MIDR[i, 0, t].astype(F32) + MIDR[i, 1, t].astype(F32)
            n = h * PAGES + j
            request = TS[8 + j, 0]
            i_page = TS[1, request]
            cos, sin = angle_at(cosp[pl.ds(i_page, 1), :], sinp[pl.ds(i_page, 1), :])
            KB[n] = normed_rope(page[:, :HD], k_gain[...], cos, sin)
            live = row < lengths[request] - i_page * ROWS
            VB[n, :, :HD] = jnp.where(live, page[:, HD:], 0.0).astype(BF16)
            VB[n, :, HD:] = jnp.where(live, 1.0, 0.0).astype(BF16)

    def attend(h, j):
        n = h * PAGES + j
        request = TS[8 + j, 0]
        core, xx, yy = lax.rem(request, 2), lax.rem(request // 2, 4), request // 8
        query = jnp.concatenate(
            [QS[h][0, core * 16 + yy * 4 + xx], QS[h][1, core * 16 + xx * 4 + yy]], axis=0
        )
        scores = nt(query, KB[n]) * SCALE
        mixed = nn(jnp.exp(scores).astype(BF16), VB[n])
        line = lax.broadcasted_iota(jnp.int32, (16, HD), 0)
        for s in range(2):
            CTX[h, j, s, :256, :] = mixed[s * 256 : (s + 1) * 256, :HD].astype(BF16)
            sums = []
            for g in range(2):
                block = mixed[s * 256 + g * ROWS : s * 256 + (g + 1) * ROWS, HD:]
                sums.append(jnp.sum(jnp.where(eye, block, 0.0), axis=0, keepdims=True))
            CTX[h, j, s, 256:, :] = jnp.where(line == 0, sums[0], jnp.where(line == 1, sums[1], 0.0)).astype(BF16)

    def attend_pages(h, first, last):
        def one(j, carry):
            attend(h, j)
            return carry

        lax.fori_loop(first, last, one, 0)

    q_at = (c * 16 + y * 4 + x, c * 16 + x * 4 + y)

    def q1_of(h, s):
        base = c * 16 + (y * 4, x * 4)[s]
        return Spread(
            lambda k: QS[h].at[s, base + k], (x, y)[s], (xall, yall)[s], lambda n: q1s.at[h, s, n], lambda n: q1r.at[h, s, n]
        )

    def q2_of(h, s):
        return Spread(
            lambda k: QS[h].at[s, pl.ds(c * 16 + k * 4, 4)], (y, x)[s], (yall, xall)[s],
            lambda n: q2s.at[h, s, n], lambda n: q2r.at[h, s, n],
        )

    q1 = [[q1_of(h, s) for s in range(2)] for h in range(2)]
    q2 = [[q2_of(h, s) for s in range(2)] for h in range(2)]

    def q3_copy(h, s, cc, n):
        ref = QS[h].at[s, pl.ds(cc * 16 + q2[h][s].places[n] * 4, 4)]
        return rcopy(ref, ref, q3s.at[h, s, n], q3r.at[h, s, n], sib)

    def angles_new():
        length = lengths[p]
        page_cos, page_sin = cosp[pl.ds(length // ROWS, 1), :], sinp[pl.ds(length // ROWS, 1), :]
        rest_cos, rest_sin = cosr[pl.ds(lax.rem(length, ROWS), 1), :], sinr[pl.ds(lax.rem(length, ROWS), 1), :]
        return angle_at(page_cos * rest_cos - page_sin * rest_sin, page_sin * rest_cos + page_cos * rest_sin)

    def q_begin():
        nh_ring.finish()
        project_new(2)
        cos_new, sin_new = angles_new()
        for h in range(2):
            for s in range(2):
                for g in range(2):
                    n = h * GROUP + s * 2 + g
                    raw = ACC[:, n * HD : (n + 1) * HD]
                    QS[h][s, q_at[s], g * ROWS : (g + 1) * ROWS, :] = normed_rope(raw, q_gain[...], cos_new, sin_new)
                q1[h][s].start()

    def q_along(h):
        for s in range(2):
            for n in range(3):
                q1[h][s].wait(n)
            q2[h][s].start()
            q3_copy(h, s, c, 0).start()

    def q_share(h):
        for n in range(3):
            for s in range(2):
                q2[h][s].wait(n)
                q3_copy(h, s, c, n + 1).start()

    def q_wait(h):
        for s in range(2):
            for n in range(4):
                q3_copy(h, s, oc, n).wait_recv()

    def attend_new():
        cos_new, sin_new = angles_new()
        causal = lax.broadcasted_iota(jnp.int32, (QROWS, ROWS), 1) <= (
            lax.broadcasted_iota(jnp.int32, (QROWS, ROWS), 0) & (ROWS - 1)
        )
        ones = jnp.ones((ROWS, HD), BF16)
        for h in range(2):
            key = normed_rope(ACC[:, 1024 + h * HD : 1024 + (h + 1) * HD], k_gain[...], cos_new, sin_new)
            val = ACC[:, 1280 + h * HD : 1280 + (h + 1) * HD].astype(BF16)
            query = jnp.concatenate([QS[h][0, q_at[0]], QS[h][1, q_at[1]]], axis=0)
            scores = nt(query, key) * SCALE
            weights = jnp.where(causal, jnp.exp(scores), 0.0).astype(BF16)
            NEWCTX[h] = nn(weights, jnp.concatenate([val, ones], axis=1))

    first_dev = ((xup, xdn), (yup, ydn))
    last_dev = (yall, xall)
    first_at, last_at = (x, y), (y, x)

    def mine(h, s, o, b, core):
        a = rot(first_at[s], o)
        chip = b * 4 + a if s == 0 else a * 4 + b
        return CTX[h, TS[0, chip * 2 + core], s]

    def value(h, s, o, b):
        return mine(h, s, o, b, c) + R0[h, s, o, b]

    def c0_copy(h, s, o):
        return rcopy(S0.at[s, o], R0.at[h, s, o], c0s.at[h, s, o], c0r.at[h, s, o], sib)

    def c0(h):
        for o in (2, 1, 3, 0):
            for s in range(2):

                def fill(b, carry):
                    S0[s, o, b] = mine(h, s, o, b, oc)
                    return carry

                lax.fori_loop(0, 4, fill, 0)
                c0_copy(h, s, o).start()

    def c1o_copy(h, s, d):
        part = pl.ds(d * 2, 2)
        return rcopy(S1O.at[h, s, part], R1O.at[h, s, part], c1os.at[h, s, d], c1or.at[h, s, d], first_dev[s][d])

    def c1m_copy(h, s, d, n):
        part = pl.ds(n * 2, 2)
        return rcopy(
            S1M.at[h, s, d, part], R1M.at[h, s, d, part], c1ms.at[h, s, d, n], c1mr.at[h, s, d, n], first_dev[s][d]
        )

    def c2_copy(h, s, n):
        src = A1.at[h, s, (1, 3, 2)[n]]
        return rcopy(src, R2M.at[h, s, n], c2s.at[h, s, n], c2r.at[h, s, n], last_dev[s][n])

    def c1(h):
        for s in range(2):
            c0_copy(h, s, 2).wait_recv()

            def fill(b, carry):
                S1O[h, s, b] = value(h, s, 2, b)
                return carry

            lax.fori_loop(0, 4, fill, 0)
            for d in range(2):
                c1o_copy(h, s, d).start()
        for d in range(2):
            for s in range(2):
                o, n = (1, 3)[d], 1 - d
                c0_copy(h, s, o).wait_recv()

                def fill(b, carry):
                    S1M[h, s, d, b] = value(h, s, o, b)
                    return carry

                lax.fori_loop(n * 2, n * 2 + 2, fill, 0)
                c1m_copy(h, s, d, n).start()

    def c2(h):
        for d in range(2):
            for s in range(2):
                o = (1, 3)[d]
                c1o_copy(h, s, d).wait_recv()

                def fill(b, carry):
                    S1M[h, s, d, b] = value(h, s, o, b) + R1O[h, s, b]
                    return carry

                lax.fori_loop(d * 2, d * 2 + 2, fill, 0)
                c1m_copy(h, s, d, d).start()

    def c3(h):
        for s in range(2):
            c0_copy(h, s, 0).wait_recv()
            for d in range(2):
                for n in range(2):
                    c1m_copy(h, s, d, n).wait_recv()

            for n, o in ((2, 2), (0, 1), (1, 3), (None, 0)):
                b = rot(last_at[s], o)
                A1[h, s, o] = value(h, s, 0, b) + R1M[h, s, 0, b] + R1M[h, s, 1, b]
                if n is not None:
                    c2_copy(h, s, n).start()

    def c4(h):
        for s in range(2):
            for n in range(3):
                c2_copy(h, s, n).wait_recv()
            parts = R2M[h, s, 0].astype(F32) + R2M[h, s, 1].astype(F32) + R2M[h, s, 2].astype(F32)
            FIN[...] = A1[h, s, 0].astype(F32) + parts
            for g in range(2):
                n = s * 2 + g
                mixed = FIN[g * ROWS : (g + 1) * ROWS, :] + NEWCTX[h, n * ROWS : (n + 1) * ROWS, :HD]
                sums = jnp.sum(jnp.where(eye, FIN[256 + g : 257 + g, :], 0.0), axis=1, keepdims=True)
                sums = sums + NEWCTX[h, n * ROWS : (n + 1) * ROWS, HD:]
                m = h * GROUP + n
                out[:, m * HD : (m + 1) * HD] = (mixed / sums).astype(BF16)

    opposite(0)
    opposite(1)
    project_new(1)
    project_new(3)

    def drain_start():
        for kv in range(2):
            for h in range(2):
                for e in (1, 2, 3):
                    w1_copy(e, h, kv).wait_send()
                w_spread[h][kv].drain()
                for n in range(4):
                    w3_copy(h, kv, c, n).wait_send()
        nh_ring.drain()
        for e in (1, 2, 3):
            rcopy(SSQ.at[z], SSQ.at[z], sqs.at[e], sqr.at[e], zdev[e]).wait_send()

    def drain_queries():
        for h in range(2):
            for s in range(2):
                q1[h][s].drain()
                q2[h][s].drain()
                for n in range(4):
                    q3_copy(h, s, c, n).wait_send()

    def drain_pages():
        def one(i, carry):
            for s in range(2):
                opp_copy(i, s).wait_send()
                mid_copy(i, s).wait_send()
            return carry

        lax.fori_loop(0, ITEMS, one, 0)

    def drain_c0(h):
        for o in range(4):
            for s in range(2):
                c0_copy(h, s, o).wait_send()

    def drain_c1(h):
        for s in range(2):
            for d in range(2):
                c1o_copy(h, s, d).wait_send()
                for n in range(2):
                    c1m_copy(h, s, d, n).wait_send()

    def drain_c2(h):
        for s in range(2):
            for n in range(3):
                c2_copy(h, s, n).wait_send()

    def step(i, carry):
        def at_step(k, *actions):
            @pl.when(i == k)
            def _():
                for action in actions:
                    action()

        @pl.when(i < ITEMS - 2)
        def _():
            opposite(i + 2)

        @pl.when(i < ITEMS)
        def _():
            neighbours(i)

        @pl.when(i >= 2)
        def _():
            own(i - 2)

        def pages(h, first, last):
            return lambda: attend_pages(h, first, last)

        def of(stage, h):
            return lambda: stage(h)

        at_step(0, q_begin)
        at_step(1, of(w_share, 1))
        at_step(2, of(q_along, 0))
        at_step(3, of(w_wait, 1), attend_new)
        at_step(4, of(q_along, 1))
        at_step(5, of(q_share, 0))
        at_step(6, of(q_wait, 0), pages(0, 0, 6))
        at_step(7, pages(0, 6, 12), of(c0, 0))
        at_step(8, of(c1, 0), of(q_share, 1))
        at_step(9, of(q_wait, 1), pages(1, 0, 3))
        at_step(10, of(c2, 0), pages(1, 3, 6))
        at_step(11, pages(1, 6, 8))
        at_step(12, of(drain_c0, 0), of(c3, 0), pages(1, 8, 10))
        at_step(13, pages(1, 10, 12))
        return carry

    lax.fori_loop(0, ITEMS + 2, step, 0)
    c0(1)
    c1(1)
    drain_start()
    c4(0)
    drain_c1(0)
    c2(1)
    drain_queries()
    drain_pages()
    drain_c2(0)
    c3(1)
    drain_c0(1)
    drain_c1(1)
    c4(1)
    drain_c2(1)


def local(store, new_hidden, wq, wk, wv, norm_gain, q_gain, k_gain, page_table, hist_len):
    tables = [jnp.asarray(t) for t in rope_tables()]
    vm = pl.BlockSpec(memory_space=pltpu.VMEM)
    hbm = pl.BlockSpec(memory_space=pl.ANY)
    dma = pltpu.SemaphoreType.DMA
    scratch = [
        pltpu.VMEM((PAGES, ROWS, FEAT), BF16),
        pltpu.VMEM((4, 2, 2, FEAT, HD), BF16),
        pltpu.VMEM((2, FEAT, 1024), BF16),
        pltpu.VMEM((2, FEAT, 256), BF16),
        pltpu.VMEM((2, FEAT, 256), BF16),
        pltpu.VMEM((ROWS, 1536), F32),
        pltpu.VMEM((4, ROWS, FEAT), BF16),
        pltpu.VMEM((4, 16, ROWS), F32),
        pltpu.VMEM((ROWS, ROWS), F32),
        pltpu.VMEM((ITEMS, 2, ROWS, 256), BF16),
        pltpu.VMEM((ITEMS, 2, ROWS, 256), BF16),
        pltpu.VMEM((ITEMS, 2, 2, ROWS, 256), BF16),
        pltpu.VMEM((ITEMS, 2, 2, ROWS, 256), BF16),
        pltpu.VMEM((2 * PAGES, ROWS, HD), BF16),
        pltpu.VMEM((2 * PAGES, ROWS, 2 * HD), BF16),
        pltpu.VMEM((2, QROWS, 2 * HD), F32),
        pltpu.VMEM((2, REQS, QROWS // 2, HD), BF16),
        pltpu.VMEM((2, REQS, QROWS // 2, HD), BF16),
        pltpu.VMEM((2, PAGES + 1, 2, HALF, HD), BF16),
        pltpu.VMEM((2, 4, 4, HALF, HD), BF16),
        pltpu.VMEM((2, 2, 4, 4, HALF, HD), BF16),
        pltpu.VMEM((2, 2, 4, HALF, HD), BF16),
        pltpu.VMEM((2, 2, 4, HALF, HD), BF16),
        pltpu.VMEM((2, 2, 2, 4, HALF, HD), BF16),
        pltpu.VMEM((2, 2, 2, 4, HALF, HD), BF16),
        pltpu.VMEM((2, 2, 4, HALF, HD), BF16),
        pltpu.VMEM((2, 2, 3, HALF, HD), BF16),
        pltpu.VMEM((HALF, HD), F32),
        pltpu.VMEM((24, HD), jnp.int32),
        pltpu.SMEM((24, HD), jnp.int32),
        pltpu.VMEM((16, REQS), jnp.int32),
        pltpu.VMEM((WIDE // HD, HD), F32),
        pltpu.VMEM((1, HD), F32),
        pltpu.VMEM((1, HD), F32),
        pltpu.VMEM((ROWS, HD), F32),
        pltpu.VMEM((ROWS, HD), F32),
        pltpu.VMEM((24, HD), F32),
        pltpu.VMEM((24, HD), F32),
        dma((16,)), dma((2, 3)),
        dma((2, 2, 4)), dma((2, 2, 4)), dma((2, 2, 4)), dma((2, 2, 4)), dma((2, 2, 4)), dma((2, 2, 4)),
        dma((4,)), dma((4,)), dma((4,)), dma((4,)),
        dma((ITEMS, 2)), dma((ITEMS, 2)), dma((ITEMS, 2)), dma((ITEMS, 2)),
        dma((2, 2, 4)), dma((2, 2, 4)), dma((2, 2, 4)), dma((2, 2, 4)), dma((2, 2, 4)), dma((2, 2, 4)),
        dma((2, 2, 4)), dma((2, 2, 4)),
        dma((2, 2, 2)), dma((2, 2, 2)), dma((2, 2, 2, 2)), dma((2, 2, 2, 2)),
        dma((2, 2, 3)), dma((2, 2, 3)),
    ]
    return pl.pallas_call(
        kernel,
        out_shape=jax.ShapeDtypeStruct((ROWS, 2 * GROUP * HD), BF16),
        in_specs=[hbm, pl.BlockSpec(memory_space=pltpu.SMEM)] + [hbm] * 12,
        out_specs=vm,
        scratch_shapes=scratch,
        compiler_params=pltpu.CompilerParams(
            collective_id=0, has_side_effects=True, vmem_limit_bytes=63 * 1024 * 1024
        ),
        cost_estimate=pl.CostEstimate(flops=12_000_000_000, bytes_accessed=25_000_000, transcendentals=2_000_000),
    )(
        page_table.T, hist_len, store, new_hidden, wq, wk, wv, norm_gain.reshape(WIDE // HD, HD),
        q_gain.reshape(1, HD), k_gain.reshape(1, HD), *tables,
    )


def solution(mesh):
    return jax.shard_map(
        local,
        mesh=mesh,
        in_specs=(
            P("pool", None, "tensor"),
            P("pool", "tensor"),
            P(None, "tensor"),
            P(None, "tensor"),
            P(None, "tensor"),
            P(),
            P(),
            P(),
            P(),
            P(),
        ),
        out_specs=P("pool", "tensor"),
        check_vma=False,
    )
```
